32 devices in a mesh: row: 4 (over y, x), col: 8 (over z, core).
Axes of the slice: x: 2, y: 2, z: 4, core: 2. Of those that a mesh axis runs over, the one named last changes fastest.
Arguments:
- tokens: bfloat16 [1024, 1152], P('row', 'col'), may hold values from -6 to 6
- cond: bfloat16 [4, 1152], P('row', 'col'), may hold values from -6 to 6
- w_mod: bfloat16 [2, 1152, 6, 1152], P(None, 'row', None, 'col'), may hold values from -0.1875 to 0.1875
- b_mod: float32 [2, 6, 1152], P(None, None, 'col'), may hold values from -1.8 to 1.8
- query_key_value_weight: bfloat16 [2, 1152, 3, 1152], P(None, 'row', None, 'col'), may hold values from -0.1875 to 0.1875
- b_qv: float32 [2, 2, 1152], P(None, None, 'col'), may hold values from -1.8 to 1.8
- attention_output_weight: bfloat16 [2, 1152, 1152], P(None, 'row', 'col'), may hold values from -0.75 to 0.75
- attention_output_bias: float32 [2, 1152], P(None, 'col'), may hold values from -1.8 to 1.8
- first_linear_weight: bfloat16 [2, 1152, 4608], P(None, 'row', 'col'), may hold values from -0.35355339 to 0.35355339
- first_linear_bias: float32 [2, 4608], P(None, 'col'), may hold values from -1.8 to 1.8
- second_linear_weight: bfloat16 [2, 4608, 1152], P(None, 'row', 'col'), may hold values from -0.09375 to 0.09375
- second_linear_bias: float32 [2, 1152], P(None, 'col'), may hold values from -1.8 to 1.8
- cotangent: bfloat16 [1024, 1152], P('row', 'col'), may hold values from -6 to 6
Outputs:
- output: bfloat16 [1024, 1152], P('row', 'col')
- grad_tokens: float32 [1024, 1152], P('row', 'col')
- grad_cond: float32 [4, 1152], P('row', 'col')
- grad_w_mod: float32 [2, 1152, 6, 1152], P(None, 'row', None, 'col')
- grad_b_mod: float32 [2, 6, 1152], P(None, None, 'col')
- grad_w_qkv: float32 [2, 1152, 3, 1152], P(None, 'row', None, 'col')
- grad_b_qv: float32 [2, 2, 1152], P(None, None, 'col')
- grad_w_out: float32 [2, 1152, 1152], P(None, 'row', 'col')
- grad_b_out: float32 [2, 1152], P(None, 'col')
- grad_w_fc1: float32 [2, 1152, 4608], P(None, 'row', 'col')
- grad_b_fc1: float32 [2, 4608], P(None, 'col')
- grad_w_fc2: float32 [2, 4608, 1152], P(None, 'row', 'col')
- grad_b_fc2: float32 [2, 1152], P(None, 'col')
The draws below stay inside these ranges and needn't reach their ends.
All inputs are finite; a program needn't handle non-finite values.
Results may differ from the reference program's by a relative error of at most 0.023.
The reference program's roundings to bfloat16 on the way count: a program that leaves them out, or rounds other values in their place, can miss the bound.
Values may be sent and summed in bfloat16 or wider, within the bound.
A program may use at most 128 MiB of HBM per device.

```python
import jax
import jax.numpy as jnp
from jax import lax

D = 1152
HEADS = 16
HEAD = 72
FF = 4608
SEQ_LEN = 256
LAYERS = 2
SEQS = 4
TOKENS = 1024


def draw_first_linear_weight(key, part):
    key = jax.random.fold_in(key, 11)
    own_key, shared_key = jax.random.split(key)
    spread = jnp.clip(jax.random.normal(own_key, (LAYERS, D, FF), jnp.float32), -6.0, 6.0) * D ** (-0.5)
    shared = jnp.clip(jax.random.normal(shared_key, (LAYERS, 1, FF), jnp.float32), -6.0, 6.0) * D ** (-0.5)
    return (spread + shared).astype(jnp.bfloat16)


def block_levels(rng, extent, cuts, smallest, top_value):
    factor_of = 1.0
    for position, shards_of in cuts:
        draws = jax.random.uniform(jax.random.fold_in(jax.random.fold_in(rng, 6), position), (shards_of,), jnp.float32, smallest / len(cuts), top_value / len(cuts))
        factor_of = factor_of * jnp.repeat(jnp.exp(draws), extent[position] // shards_of).reshape((-1,) + (1,) * (len(extent) - 1 - position))
    return factor_of


def normal_values(rng, dims, width, bound, cuts=(), held_as=jnp.bfloat16):
    factor_of = block_levels(rng, dims, cuts, -0.22, 0.18) if cuts else 1.0
    entries = jax.random.normal(rng, dims, jnp.float32) * width * factor_of
    return jnp.minimum(jnp.maximum(entries, -bound), bound).astype(held_as)


def setup_inputs(seed: int = 0) -> dict:
    keys = jax.random.split(jax.random.key(seed), 14)
    return {
        "tokens": normal_values(keys[0], (TOKENS, D), 1.0, 6.0, ((0, 4), (1, 8))),
        "cond": normal_values(keys[1], (SEQS, D), 1.0, 6.0, ((0, 4), (1, 8))),
        "w_mod": normal_values(keys[2], (LAYERS, D, 6, D), D ** -0.5, 0.1875, ((1, 4), (3, 8))),
        "b_mod": normal_values(keys[3], (LAYERS, 6, D), 0.3, 1.8, ((2, 8),), jnp.float32),
        "query_key_value_weight": normal_values(keys[4], (LAYERS, D, 3, D), D ** -0.5, 0.1875, ((1, 4), (3, 8))),
        "b_qv": normal_values(keys[5], (LAYERS, 2, D), 0.3, 1.8, ((2, 8),), jnp.float32),
        "attention_output_weight": normal_values(keys[6], (LAYERS, D, D), (D // 16) ** -0.5, 0.75, ((1, 4), (2, 8))),
        "attention_output_bias": normal_values(keys[7], (LAYERS, D), 0.3, 1.8, ((1, 8),), jnp.float32),
        "first_linear_weight": draw_first_linear_weight(jax.random.fold_in(keys[13], 71), 0),
        "first_linear_bias": normal_values(keys[9], (LAYERS, FF), 0.3, 1.8, ((1, 8),), jnp.float32),
        "second_linear_weight": normal_values(keys[10], (LAYERS, FF, D), FF ** -0.5, 0.09375, ((1, 4), (2, 8))),
        "second_linear_bias": normal_values(keys[11], (LAYERS, D), 0.3, 1.8, ((1, 8),), jnp.float32),
        "cotangent": normal_values(keys[12], (TOKENS, D), 1.0, 6.0, ((0, 4), (1, 8))),
    }


HIGH_ACCURACY = lax.Precision.HIGHEST
EPS = 1e-06

@jax.custom_vjp
def low(v):
    return lax.optimization_barrier(v.astype(jnp.bfloat16)).astype(jnp.float32)

@jax.custom_vjp
def low_back(v):
    return v

def low_keep(v):
    return (low(v), None)

def low_pass(kept, grad):
    return (grad,)

def back_keep(v):
    return (v, None)

def back_low(kept, grad):
    return (low(grad),)
low.defvjp(low_keep, low_pass)
low_back.defvjp(back_keep, back_low)

def layer_norm(values):
    average = lax.optimization_barrier(jnp.mean(values, axis=-1, keepdims=True))
    centred = values - average
    spread = lax.optimization_barrier(jnp.mean(centred * centred, axis=-1, keepdims=True))
    return centred * lax.rsqrt(spread + EPS)

def attend_one(operands):
    query_rows, key_rows, value_rows = operands
    scores = jnp.einsum('qhe,khe->hqk', query_rows, key_rows, precision=HIGH_ACCURACY) * HEAD ** (-0.5)
    scores = low_back(scores)
    probs = low(jax.nn.softmax(scores, axis=-1))
    return jnp.einsum('hqk,khe->qhe', probs, value_rows, precision=HIGH_ACCURACY)

def forward(tokens, cond, w_mod, b_mod, query_key_value_weight, b_qv, attention_output_weight, attention_output_bias, first_linear_weight, first_linear_bias, second_linear_weight, second_linear_bias):
    stream = tokens.reshape(SEQS, SEQ_LEN, D)
    signal = low(jax.nn.silu(cond))
    for layer_index in range(LAYERS):
        modulation = jnp.dot(signal, w_mod[layer_index].reshape(D, 6 * D), precision=HIGH_ACCURACY).reshape(SEQS, 6, D) + b_mod[layer_index]
        modulation = low_back(modulation)
        shift1, scale1, gate1, shift2, scale2, gate2 = [modulation[:, None, column_no] for column_no in range(6)]
        hidden_first = low(layer_norm(stream) * (1.0 + scale1) + shift1)
        query_key_value_bias = jnp.stack([b_qv[layer_index, 0], jnp.zeros_like(b_qv[layer_index, 0]), b_qv[layer_index, 1]])
        query_key_value = jnp.einsum('aib,bew->aiew', hidden_first, query_key_value_weight[layer_index], precision=HIGH_ACCURACY) + query_key_value_bias
        query_key_value = low(low_back(query_key_value))
        heads_view = query_key_value.reshape(SEQS, SEQ_LEN, 3, HEADS, HEAD)
        attended_values = lax.map(jax.checkpoint(attend_one), (heads_view[:, :, 0], heads_view[:, :, 1], heads_view[:, :, 2]))
        attended_values = low(low_back(attended_values.reshape(SEQS, SEQ_LEN, D)))
        attention_branch = low_back(jnp.einsum('nvk,kj->nvj', attended_values, attention_output_weight[layer_index], precision=HIGH_ACCURACY) + attention_output_bias[layer_index])
        stream = stream + gate1 * attention_branch
        hidden_second = low(layer_norm(stream) * (1.0 + scale2) + shift2)
        preactivation_values = low_back(jnp.einsum('nvk,kj->nvj', hidden_second, first_linear_weight[layer_index], precision=HIGH_ACCURACY) + first_linear_bias[layer_index])
        activated_hidden = low(jax.nn.gelu(preactivation_values, approximate=True))
        feedforward_branch = low_back(jnp.einsum('gez,zm->gem', activated_hidden, second_linear_weight[layer_index], precision=HIGH_ACCURACY) + second_linear_bias[layer_index])
        stream = stream + gate2 * feedforward_branch
    return stream.reshape(TOKENS, D)

def reference(tokens, cond, w_mod, b_mod, query_key_value_weight, b_qv, attention_output_weight, attention_output_bias, first_linear_weight, first_linear_bias, second_linear_weight, second_linear_bias, cotangent):
    floats = [array.astype(jnp.float32) for array in (tokens, cond, w_mod, b_mod, query_key_value_weight, b_qv, attention_output_weight, attention_output_bias, first_linear_weight, first_linear_bias, second_linear_weight, second_linear_bias)]
    output, pullback = jax.vjp(forward, *floats)
    grads = pullback(cotangent.astype(jnp.float32))
    return (output.astype(jnp.bfloat16), grads[0], grads[1], grads[2], grads[3], grads[4], grads[5], grads[6], grads[7], grads[8], grads[9], grads[10], grads[11])
```

```python
import functools
import math

import jax
import jax.numpy as jnp
from jax import lax
from jax.experimental import pallas as pl
from jax.experimental.pallas import tpu as pltpu
from jax.sharding import PartitionSpec as P

D = 1152
HEAD = 72
LAYERS = 2
EPS = 1e-06
SCALE = HEAD ** (-0.5)
BF16 = jnp.bfloat16
F32 = jnp.float32
MESH = pl.DeviceIdType.MESH
VMEM_BYTES = 52 * 1024 * 1024


def nn(a, b):
    return lax.dot_general(a, b, (((1,), (0,)), ((), ())), preferred_element_type=F32)


def tn(a, b):
    return lax.dot_general(a, b, (((0,), (0,)), ((), ())), preferred_element_type=F32)


def nt(a, b):
    return lax.dot_general(a, b, (((1,), (1,)), ((), ())), preferred_element_type=F32)


def flat(x):
    blocks, rows, columns = x.shape
    if rows % 16 == 0:
        return x.reshape(blocks * rows, columns)
    return x.astype(F32).reshape(blocks * rows, columns).astype(x.dtype)


class Place:
    def __init__(self, count):
        self.row = lax.axis_index("row")
        self.col = lax.axis_index("col")
        self.count = count
        self.zs = count // 2
        self.z = self.col // 2
        self.core = self.col % 2
        self.mate_core = 1 - self.core
        self.mate = (self.row, self.z * 2 + self.mate_core)

    def ahead(self, k):
        return lax.rem(self.z + k, self.zs)

    def behind(self, k):
        return lax.rem(self.z + self.zs - k, self.zs)

    def peer(self, z):
        return (self.row, z * 2 + self.core)


def greet(here):
    barrier = pltpu.get_barrier_semaphore()
    pl.semaphore_signal(barrier, inc=1, device_id=here.mate, device_id_type=MESH)
    for k in range(1, here.zs):
        pl.semaphore_signal(
            barrier, inc=1, device_id=here.peer(here.ahead(k)), device_id_type=MESH
        )
    pl.semaphore_wait(barrier, here.zs)


def send(src, dst, send_sem, recv_sem, device):
    return pltpu.make_async_remote_copy(
        src_ref=src,
        dst_ref=dst,
        send_sem=send_sem,
        recv_sem=recv_sem,
        device_id=device,
        device_id_type=MESH,
    )


def gather(here, buf, out_sem, fwd_sem, in_sem):
    own = here.col
    started = []
    for k in range(1, here.zs):
        copy = send(
            buf.at[own], buf.at[own], out_sem.at[k], in_sem.at[own], here.peer(here.ahead(k))
        )
        copy.start()
        started.append(copy)
    copy = send(buf.at[own], buf.at[own], out_sem.at[0], in_sem.at[own], here.mate)
    copy.start()
    started.append(copy)
    for k in range(1, here.zs):
        src = here.behind(k) * 2 + here.core
        copy = send(buf.at[src], buf.at[src], fwd_sem.at[k], in_sem.at[src], here.mate)
        copy.wait_recv()
        copy.start()
        started.append(copy)
    for k in range(here.zs):
        src = here.behind(k) * 2 + here.mate_core
        send(buf.at[src], buf.at[src], fwd_sem.at[0], in_sem.at[src], here.mate).wait_recv()
    for copy in started:
        copy.wait_send()


def scatter_sum(here, parts, near, far, near_sems, far_sems, stat=None):
    near_out, near_in = near_sems
    far_out, far_in = far_sems
    z, core = here.z, here.core
    order = list(range(1, here.zs)) + [0]
    near_copies = []
    if stat is not None:
        own, got, sums, others, stat_sems = stat
        stat_out, stat_in = stat_sems
        first = send(own, got, stat_out.at[0], stat_in.at[z], here.mate)
        first.start()
    for k in order:
        to = here.ahead(k)
        copy = send(
            parts.at[here.mate_core, to], near.at[to], near_out.at[k], near_in.at[to], here.mate
        )
        copy.start()
        near_copies.append(copy)
    far_copies = []
    if stat is not None:
        first.wait()
        sums[...] = own[...] + got[...]
        for k in range(1, here.zs):
            copy = send(
                sums, others.at[z], stat_out.at[k], stat_in.at[z], here.peer(here.ahead(k))
            )
            copy.start()
            far_copies.append(copy)
    total = None
    for i, k in enumerate(order):
        to = here.ahead(k)
        near_copies[i].wait_recv()
        both = parts[core, to].astype(F32) + near[to].astype(F32)
        if k == 0:
            total = both
        else:
            parts[core, to] = both.astype(BF16)
            copy = send(
                parts.at[core, to], far.at[z], far_out.at[k], far_in.at[z], here.peer(to)
            )
            copy.start()
            far_copies.append(copy)
    stat_total = None
    if stat is not None:
        stat_total = sums[...]
        for k in range(1, here.zs):
            src = here.behind(k)
            send(
                sums, others.at[src], stat_out.at[k], stat_in.at[src], here.peer(src)
            ).wait_recv()
            stat_total = stat_total + others[src]
    for k in range(1, here.zs):
        src = here.behind(k)
        send(
            parts.at[core, src], far.at[src], far_out.at[k], far_in.at[src], here.peer(src)
        ).wait_recv()
        total = total + far[src].astype(F32)
    for copy in near_copies:
        copy.wait_send()
    for copy in far_copies:
        copy.wait_send()
    return total, stat_total


def normalize(stream):
    average = jnp.sum(stream, 0, keepdims=True) / D
    centred = stream - average
    spread = jnp.sum(centred * centred, 0, keepdims=True) / D
    inverse = lax.rsqrt(spread + EPS)
    return centred * inverse, inverse


def gelu(u):
    inner = math.sqrt(2 / math.pi) * (u + 0.044715 * (u * u * u))
    return 0.5 * u * (1.0 + jnp.tanh(inner))


def gelu_slope(u):
    root = math.sqrt(2 / math.pi)
    t = jnp.tanh(root * (u + 0.044715 * (u * u * u)))
    return 0.5 * (1.0 + t) + 0.5 * u * (1.0 - t * t) * (root * (1.0 + 3 * 0.044715 * (u * u)))


def attention_forward(
    count, stream, mod, mod_own, w_qkv, b_qkv, w_out, b_out,
    normed, inverse, hidden, qkv, log_total, attended, branch, stream_out,
    x_buf, a_buf, x_out, x_fwd, x_in, a_out, a_fwd, a_in,
):
    here = Place(count)
    greet(here)
    x_buf[here.col] = stream[...].astype(BF16)
    gather(here, x_buf, x_out, x_fwd, x_in)
    values, inv = normalize(flat(x_buf[...]).astype(F32))
    normed[...] = values
    inverse[...] = inv
    hidden_now = (values * (1.0 + mod[:, 1:2]) + mod[:, 0:1]).astype(BF16)
    hidden[...] = hidden_now
    projected = tn(flat(w_qkv[...]), hidden_now) + b_qkv[...]
    heads = qkv.shape[0] // 3
    for i in range(3 * heads):
        qkv[i] = projected[i * HEAD : (i + 1) * HEAD].astype(BF16)
    pieces = []
    for h in range(heads):
        scores = tn(qkv[heads + h], qkv[h]) * SCALE
        highest = jnp.max(scores, axis=0, keepdims=True)
        expd = jnp.exp(scores - highest)
        summed = jnp.sum(expd, axis=0, keepdims=True)
        log_total[h] = highest + jnp.log(summed)
        probs = (expd / summed).astype(BF16)
        pieces.append(nn(qkv[2 * heads + h], probs))
    a_buf[here.col] = jnp.concatenate(pieces, axis=0).astype(BF16)
    gather(here, a_buf, a_out, a_fwd, a_in)
    attended_now = flat(a_buf[...])
    attended[...] = attended_now
    branch_now = tn(flat(w_out[...]), attended_now) + b_out[...]
    branch[...] = branch_now
    stream_out[...] = stream[...] + mod_own[:, 2:3] * branch_now


def mlp_forward(
    count, stream, mod, mod_own, w_one, b_one, w_two, b_two,
    normed, inverse, hidden, pre, activated, branch, stream_out,
    x_buf, a_buf, x_out, x_fwd, x_in, a_out, a_fwd, a_in,
):
    here = Place(count)
    greet(here)
    x_buf[here.col] = stream[...].astype(BF16)
    gather(here, x_buf, x_out, x_fwd, x_in)
    values, inv = normalize(flat(x_buf[...]).astype(F32))
    normed[...] = values
    inverse[...] = inv
    hidden_now = (values * (1.0 + mod[:, 4:5]) + mod[:, 3:4]).astype(BF16)
    hidden[...] = hidden_now
    pre_now = tn(flat(w_one[...]), hidden_now) + b_one[...]
    pre[...] = pre_now
    a_buf[here.col] = gelu(pre_now).astype(BF16)
    gather(here, a_buf, a_out, a_fwd, a_in)
    activated_now = flat(a_buf[...])
    activated[...] = activated_now
    branch_now = tn(flat(w_two[...]), activated_now) + b_two[...]
    branch[...] = branch_now
    stream_out[...] = stream[...] + mod_own[:, 5:6] * branch_now


def split_parts(here, parts, weight, rows):
    for c in range(here.count):
        parts[c % 2, c // 2] = nn(weight[c], rows).astype(BF16)


def split_norm_parts(here, parts, stat, weight, rows, normed, gain):
    width = weight.shape[1]
    plain = crossed = 0.0
    for c in range(here.count):
        block = nn(weight[c], rows)
        parts[c % 2, c // 2] = block.astype(BF16)
        span = slice(c * width, (c + 1) * width)
        scaled = block * (1.0 + gain[span])
        plain = plain + jnp.sum(scaled, 0, keepdims=True)
        crossed = crossed + jnp.sum(scaled * normed[span], 0, keepdims=True)
    stat[0:1] = plain
    stat[1:2] = crossed


def norm_back(here, grad_hidden, totals, normed, inverse, gain):
    width = grad_hidden.shape[0]
    own = normed[pl.ds(pl.multiple_of(here.col * width, 8), width)]
    scaled = grad_hidden * (1.0 + gain)
    change = inverse[...] * (scaled - totals[0:1] / D - own * (totals[1:2] / D))
    shift = jnp.sum(grad_hidden, 1, keepdims=True)
    stretch = jnp.sum(grad_hidden * own, 1, keepdims=True)
    return change, shift, stretch


def mlp_backward(
    count, grad, mod, mod_own, branch, pre, normed, inverse, w_one, w_two,
    grad_branch, grad_pre, grad_out, sums, sums_pre,
    a_parts, a_near, a_far, h_parts, h_near, h_far, stat_own, stat_got, stat_sum, stat_far,
    an_out, an_in, af_out, af_in, hn_out, hn_in, hf_out, hf_in, st_out, st_in,
):
    here = Place(count)
    greet(here)
    grad_now = grad[...]
    grad_branch_now = (mod_own[:, 5:6] * grad_now).astype(BF16)
    grad_branch[...] = grad_branch_now
    split_parts(here, a_parts, w_two, grad_branch_now)
    grad_act, _ = scatter_sum(
        here, a_parts, a_near, a_far, (an_out, an_in), (af_out, af_in)
    )
    grad_pre_now = (grad_act * gelu_slope(pre[...])).astype(BF16)
    grad_pre[...] = grad_pre_now
    stat_own[...] = jnp.zeros_like(stat_own)
    split_norm_parts(here, h_parts, stat_own, w_one, grad_pre_now, normed, mod[:, 4:5])
    grad_hidden, totals = scatter_sum(
        here, h_parts, h_near, h_far, (hn_out, hn_in), (hf_out, hf_in),
        (stat_own, stat_got, stat_sum, stat_far, (st_out, st_in)),
    )
    change, shift, stretch = norm_back(
        here, grad_hidden, totals, normed, inverse, mod_own[:, 4:5]
    )
    grad_out[...] = grad_now + change
    sums[:, 0:1] = shift
    sums[:, 1:2] = stretch
    sums[:, 2:3] = jnp.sum(grad_now * branch[...], 1, keepdims=True)
    sums[:, 3:4] = jnp.sum(grad_branch_now.astype(F32), 1, keepdims=True)
    sums_pre[...] = jnp.sum(grad_pre_now.astype(F32), 1, keepdims=True)


def attention_backward(
    count, grad, mod, mod_own, branch, qkv, log_total, normed, inverse, w_qkv, w_out,
    grad_branch, grad_qkv, grad_out, sums, sums_qkv,
    a_parts, a_near, a_far, h_parts, h_near, h_far, stat_own, stat_got, stat_sum, stat_far,
    an_out, an_in, af_out, af_in, hn_out, hn_in, hf_out, hf_in, st_out, st_in,
):
    here = Place(count)
    greet(here)
    grad_now = grad[...]
    grad_branch_now = (mod_own[:, 2:3] * grad_now).astype(BF16)
    grad_branch[...] = grad_branch_now
    split_parts(here, a_parts, w_out, grad_branch_now)
    grad_att, _ = scatter_sum(
        here, a_parts, a_near, a_far, (an_out, an_in), (af_out, af_in)
    )
    heads = qkv.shape[0] // 3
    queries, keys, values = [], [], []
    for h in range(heads):
        query, key, value = qkv[h], qkv[heads + h], qkv[2 * heads + h]
        grad_one = grad_att[h * HEAD : (h + 1) * HEAD].astype(BF16)
        weights = jnp.exp(tn(key, query) * SCALE - log_total[h])
        grad_weights = tn(value, grad_one)
        values.append(nt(grad_one, weights.astype(BF16)))
        inner = jnp.sum(weights * grad_weights, axis=0, keepdims=True)
        grad_scores = (weights * (grad_weights - inner)).astype(BF16)
        queries.append(nn(key, grad_scores) * SCALE)
        keys.append(nt(query, grad_scores) * SCALE)
    grad_qkv_now = jnp.concatenate(queries + keys + values, axis=0).astype(BF16)
    grad_qkv[...] = grad_qkv_now
    stat_own[...] = jnp.zeros_like(stat_own)
    split_norm_parts(here, h_parts, stat_own, w_qkv, grad_qkv_now, normed, mod[:, 1:2])
    grad_hidden, totals = scatter_sum(
        here, h_parts, h_near, h_far, (hn_out, hn_in), (hf_out, hf_in),
        (stat_own, stat_got, stat_sum, stat_far, (st_out, st_in)),
    )
    change, shift, stretch = norm_back(
        here, grad_hidden, totals, normed, inverse, mod_own[:, 1:2]
    )
    grad_out[...] = grad_now + change
    sums[:, 0:1] = shift
    sums[:, 1:2] = stretch
    sums[:, 2:3] = jnp.sum(grad_now * branch[...], 1, keepdims=True)
    sums[:, 3:4] = jnp.sum(grad_branch_now.astype(F32), 1, keepdims=True)
    sums_qkv[...] = jnp.sum(grad_qkv_now.astype(F32), 1, keepdims=True)


def run(body, ident, count, args, outs, scratch):
    vmem = pl.BlockSpec(memory_space=pltpu.VMEM)
    return pl.pallas_call(
        functools.partial(body, count),
        out_shape=[jax.ShapeDtypeStruct(shape, dtype) for shape, dtype in outs],
        in_specs=[vmem] * len(args),
        out_specs=[vmem] * len(outs),
        scratch_shapes=scratch,
        compiler_params=pltpu.CompilerParams(
            collective_id=ident, has_side_effects=True, vmem_limit_bytes=VMEM_BYTES
        ),
        cost_estimate=pl.CostEstimate(
            flops=2_000_000_000, bytes_accessed=60_000_000, transcendentals=0
        ),
    )(*args)


def gather_scratch(count, sizes, width):
    bufs = [pltpu.VMEM((count, size, width), BF16) for size in sizes]
    sems = [pltpu.SemaphoreType.DMA((count,)) for _ in range(3 * len(sizes))]
    return bufs + sems


def scatter_scratch(count, sizes, width):
    zs = count // 2
    bufs = []
    for size in sizes:
        bufs.append(pltpu.VMEM((2, zs, size, width), BF16))
        bufs.append(pltpu.VMEM((zs, size, width), BF16))
        bufs.append(pltpu.VMEM((zs, size, width), BF16))
    bufs += [pltpu.VMEM((8, width), F32) for _ in range(3)]
    bufs.append(pltpu.VMEM((zs, 8, width), F32))
    sems = [pltpu.SemaphoreType.DMA((zs,)) for _ in range(4 * len(sizes) + 2)]
    return bufs + sems


def weight_grad(gathered, grad_rows):
    product = lax.dot_general(
        gathered, grad_rows, (((1,), (1,)), ((), ())), preferred_element_type=F32
    )
    return lax.psum_scatter(
        product.astype(BF16), "row", scatter_dimension=0, tiled=True
    ).astype(F32)


def whole_rows(weight, count):
    full = lax.all_gather(weight, "row", axis=0, tiled=True)
    return full.reshape(count, full.shape[0] // count, full.shape[1])


def per_device(
    count,
    tokens, cond, w_mod, b_mod, query_key_value_weight, b_qv,
    attention_output_weight, attention_output_bias, first_linear_weight, first_linear_bias,
    second_linear_weight, second_linear_bias, cotangent,
):
    seq_count = cond.shape[0]
    assert seq_count == 1
    length, width = tokens.shape
    heads = width // HEAD
    hidden_width = first_linear_weight.shape[2]
    rows_in = w_mod.shape[1]
    row_index = lax.axis_index("row")
    cond_float = cond.astype(F32)
    signal = jax.nn.silu(cond_float).astype(BF16)
    signal_all = lax.all_gather(
        lax.all_gather(signal, "col", axis=1, tiled=True), "row", axis=0, tiled=True
    )
    signal_part = lax.dynamic_slice_in_dim(signal_all, row_index * rows_in, rows_in, 1)
    mod_parts = jnp.stack(
        [
            jnp.dot(signal_part, w_mod[i].reshape(rows_in, -1), preferred_element_type=F32)
            for i in range(LAYERS)
        ],
        axis=1,
    )
    mod_own = lax.psum_scatter(mod_parts, "row", scatter_dimension=0, tiled=True)
    mod_own = mod_own.reshape(LAYERS, 6, width) + b_mod
    mod_own = jnp.swapaxes(mod_own, 1, 2)
    mod_full = lax.all_gather(mod_own, "col", axis=1, tiled=True)

    weights = []
    for i in range(LAYERS):
        weights.append(
            (
                whole_rows(query_key_value_weight[i].reshape(rows_in, -1), count),
                whole_rows(attention_output_weight[i], count),
                whole_rows(first_linear_weight[i], count),
                whole_rows(second_linear_weight[i], count),
            )
        )

    stream = tokens.astype(F32).T
    saved = []
    for i in range(LAYERS):
        w_qkv, w_out, w_one, w_two = weights[i]
        bias = jnp.concatenate([b_qv[i, 0], jnp.zeros_like(b_qv[i, 0]), b_qv[i, 1]])[:, None]
        normed1, inverse1, hidden1, qkv, log_total, attended, branch1, stream = run(
            attention_forward, 0, count,
            (
                stream, mod_full[i], mod_own[i], w_qkv, bias, w_out,
                attention_output_bias[i][:, None],
            ),
            [
                ((D, length), F32),
                ((1, length), F32),
                ((D, length), BF16),
                ((3 * heads, HEAD, length), BF16),
                ((heads, 1, length), F32),
                ((D, length), BF16),
                ((width, length), F32),
                ((width, length), F32),
            ],
            gather_scratch(count, (width, width), length),
        )
        normed2, inverse2, hidden2, pre, activated, branch2, stream = run(
            mlp_forward, 1, count,
            (
                stream, mod_full[i], mod_own[i], w_one, first_linear_bias[i][:, None], w_two,
                second_linear_bias[i][:, None],
            ),
            [
                ((D, length), F32),
                ((1, length), F32),
                ((D, length), BF16),
                ((hidden_width, length), F32),
                ((count * hidden_width, length), BF16),
                ((width, length), F32),
                ((width, length), F32),
            ],
            gather_scratch(count, (width, hidden_width), length),
        )
        saved.append(
            (
                normed1, inverse1, hidden1, qkv, log_total, attended, branch1,
                normed2, inverse2, hidden2, pre, activated, branch2,
            )
        )
    output = stream.T.astype(BF16)

    grad = cotangent.astype(F32).T
    signal_back = jnp.zeros((signal_all.shape[0], rows_in), F32)
    results = {}
    for i in reversed(range(LAYERS)):
        w_qkv, w_out, w_one, w_two = weights[i]
        (
            normed1, inverse1, hidden1, qkv, log_total, attended, branch1,
            normed2, inverse2, hidden2, pre, activated, branch2,
        ) = saved[i]
        grad_branch2, grad_pre, grad, sums2, sums_pre = run(
            mlp_backward, 2, count,
            (grad, mod_full[i], mod_own[i], branch2, pre, normed2, inverse2, w_one, w_two),
            [
                ((width, length), BF16),
                ((hidden_width, length), BF16),
                ((width, length), F32),
                ((width, 4), F32),
                ((hidden_width, 1), F32),
            ],
            scatter_scratch(count, (hidden_width, width), length),
        )
        grad_fc2 = weight_grad(activated, grad_branch2)
        grad_fc1 = weight_grad(hidden2, grad_pre)
        grad_branch1, grad_qkv, grad, sums1, sums_qkv = run(
            attention_backward, 3, count,
            (
                grad, mod_full[i], mod_own[i], branch1, qkv, log_total, normed1, inverse1,
                w_qkv, w_out,
            ),
            [
                ((width, length), BF16),
                ((3 * width, length), BF16),
                ((width, length), F32),
                ((width, 4), F32),
                ((3 * width, 1), F32),
            ],
            scatter_scratch(count, (width, width), length),
        )
        grad_out_w = weight_grad(attended, grad_branch1)
        grad_qkv_w = weight_grad(hidden1, grad_qkv).reshape(-1, 3, width)
        grad_mod = jnp.concatenate([sums1[:, 0:3], sums2[:, 0:3]], axis=1).T.astype(BF16)
        grad_mod_all = lax.all_gather(
            grad_mod.reshape(1, 6 * width), "row", axis=0, tiled=True
        )
        grad_mod_w = lax.dot_general(
            signal_part, grad_mod_all, (((0,), (0,)), ((), ())), preferred_element_type=F32
        ).reshape(-1, 6, width)
        signal_back = signal_back + lax.dot_general(
            grad_mod_all,
            w_mod[i].reshape(rows_in, -1),
            (((1,), (1,)), ((), ())),
            preferred_element_type=F32,
        )
        bias_mod = jnp.sum(grad_mod_all.astype(F32), 0).reshape(6, width)
        biases = (
            jnp.stack([sums_qkv[:width, 0], sums_qkv[2 * width :, 0]]),
            sums1[:, 3],
            sums_pre[:, 0],
            sums2[:, 3],
        )
        results[i] = (grad_mod_w, bias_mod, grad_qkv_w, grad_out_w, grad_fc1, grad_fc2, biases)
    bias_sums = lax.psum([results[i][6] for i in range(LAYERS)], "row")
    signal_back = lax.psum(signal_back, "col")
    signal_back = lax.all_gather(signal_back, "row", axis=1, tiled=True)
    grad_signal = lax.dynamic_slice(
        signal_back,
        (row_index * seq_count, lax.axis_index("col") * width),
        (seq_count, width),
    )
    grad_cond = jax.vjp(jax.nn.silu, cond_float)[1](grad_signal)[0]

    def stacked(member):
        return jnp.stack([results[i][member] for i in range(LAYERS)])

    def stacked_bias(member):
        return jnp.stack([bias_sums[i][member] for i in range(LAYERS)])

    return (
        output,
        grad.T,
        grad_cond,
        stacked(0),
        stacked(1),
        stacked(2),
        stacked_bias(0),
        stacked(3),
        stacked_bias(1),
        stacked(4),
        stacked_bias(2),
        stacked(5),
        stacked_bias(3),
    )


def solution(mesh):
    in_specs = (
        P("row", "col"),
        P("row", "col"),
        P(None, "row", None, "col"),
        P(None, None, "col"),
        P(None, "row", None, "col"),
        P(None, None, "col"),
        P(None, "row", "col"),
        P(None, "col"),
        P(None, "row", "col"),
        P(None, "col"),
        P(None, "row", "col"),
        P(None, "col"),
        P("row", "col"),
    )
    out_specs = (
        P("row", "col"),
        P("row", "col"),
        P("row", "col"),
        P(None, "row", None, "col"),
        P(None, None, "col"),
        P(None, "row", None, "col"),
        P(None, None, "col"),
        P(None, "row", "col"),
        P(None, "col"),
        P(None, "row", "col"),
        P(None, "col"),
        P(None, "row", "col"),
        P(None, "col"),
    )
    return jax.shard_map(
        functools.partial(per_device, mesh.shape["col"]),
        mesh=mesh,
        in_specs=in_specs,
        out_specs=out_specs,
        check_vma=False,
    )
```

```python
import functools
import math

import jax
import jax.numpy as jnp
from jax import lax
from jax.experimental import pallas as pl
from jax.experimental.pallas import tpu as pltpu
from jax.sharding import PartitionSpec as P

D = 1152
HEAD = 72
LAYERS = 2
EPS = 1e-06
SCALE = HEAD ** (-0.5)
BF16 = jnp.bfloat16
F32 = jnp.float32
MESH = pl.DeviceIdType.MESH
VMEM_BYTES = 52 * 1024 * 1024


def nn(a, b):
    return lax.dot_general(a, b, (((1,), (0,)), ((), ())), preferred_element_type=F32)


def tn(a, b):
    return lax.dot_general(a, b, (((0,), (0,)), ((), ())), preferred_element_type=F32)


def nt(a, b):
    return lax.dot_general(a, b, (((1,), (1,)), ((), ())), preferred_element_type=F32)


def flat(x):
    blocks, rows, columns = x.shape
    if rows % 16 == 0:
        return x.reshape(blocks * rows, columns)
    return x.astype(F32).reshape(blocks * rows, columns).astype(x.dtype)


class Place:
    def __init__(self, sizes):
        rows, count = sizes
        self.rows = rows
        self.per_row = count // rows
        self.row = lax.axis_index("row")
        self.col = lax.axis_index("col")
        self.count = count
        self.zs = count // 2
        self.z = self.col // 2
        self.core = self.col % 2
        self.mate_core = 1 - self.core
        self.mate = (self.row, self.z * 2 + self.mate_core)

    def ahead(self, k):
        return lax.rem(self.z + k, self.zs)

    def behind(self, k):
        return lax.rem(self.z + self.zs - k, self.zs)

    def peer(self, z):
        return (self.row, z * 2 + self.core)

    def below(self, k):
        return lax.rem(self.row + k, self.rows)

    def above(self, k):
        return lax.rem(self.row + self.rows - k, self.rows)


def greet(here, with_rows=True):
    barrier = pltpu.get_barrier_semaphore()
    pl.semaphore_signal(barrier, inc=1, device_id=here.mate, device_id_type=MESH)
    for k in range(1, here.zs):
        pl.semaphore_signal(
            barrier, inc=1, device_id=here.peer(here.ahead(k)), device_id_type=MESH
        )
    if with_rows:
        for k in range(1, here.rows):
            pl.semaphore_signal(
                barrier, inc=1, device_id=(here.below(k), here.col), device_id_type=MESH
            )
        pl.semaphore_wait(barrier, here.zs + here.rows - 1)
    else:
        pl.semaphore_wait(barrier, here.zs)


def send(src, dst, send_sem, recv_sem, device):
    return pltpu.make_async_remote_copy(
        src_ref=src,
        dst_ref=dst,
        send_sem=send_sem,
        recv_sem=recv_sem,
        device_id=device,
        device_id_type=MESH,
    )


def gather(here, buf, out_sem, fwd_sem, in_sem):
    own = here.col
    started = []
    for k in range(1, here.zs):
        copy = send(
            buf.at[own], buf.at[own], out_sem.at[k], in_sem.at[own], here.peer(here.ahead(k))
        )
        copy.start()
        started.append(copy)
    copy = send(buf.at[own], buf.at[own], out_sem.at[0], in_sem.at[own], here.mate)
    copy.start()
    started.append(copy)
    for k in range(1, here.zs):
        src = here.behind(k) * 2 + here.core
        copy = send(buf.at[src], buf.at[src], fwd_sem.at[k], in_sem.at[src], here.mate)
        copy.wait_recv()
        copy.start()
        started.append(copy)
    for k in range(here.zs):
        src = here.behind(k) * 2 + here.mate_core
        send(buf.at[src], buf.at[src], fwd_sem.at[0], in_sem.at[src], here.mate).wait_recv()
    for copy in started:
        copy.wait_send()


class RowGather:
    def __init__(self, here, src, dst, sems):
        self.here, self.src, self.dst = here, src, dst
        self.out, self.into = sems.at[0], sems.at[1]
        own = here.row
        self.local = pltpu.make_async_copy(src, dst.at[own], self.out.at[0])
        self.local.start()
        self.copies = []
        for k in range(1, here.rows):
            copy = send(
                src, dst.at[own], self.out.at[k], self.into.at[own], (here.below(k), here.col)
            )
            copy.start()
            self.copies.append(copy)

    def finish(self):
        here = self.here
        self.local.wait()
        for k in range(1, here.rows):
            src = here.above(k)
            send(
                self.src, self.dst.at[src], self.out.at[k], self.into.at[src], (src, here.col)
            ).wait_recv()
        for copy in self.copies:
            copy.wait_send()


class RowSum:
    def __init__(self, here, parts, got, sems):
        self.here, self.parts, self.got = here, parts, got
        self.out, self.into = sems.at[0], sems.at[1]
        self.copies = []
        for k in range(1, here.rows):
            to = here.below(k)
            copy = send(
                parts.at[to],
                got.at[here.row],
                self.out.at[k],
                self.into.at[here.row],
                (to, here.col),
            )
            copy.start()
            self.copies.append(copy)

    def finish(self):
        here = self.here
        total = self.parts[here.row].astype(F32)
        for k in range(1, here.rows):
            src = here.above(k)
            send(
                self.parts.at[src],
                self.got.at[src],
                self.out.at[k],
                self.into.at[src],
                (src, here.col),
            ).wait_recv()
            total = total + self.got[src].astype(F32)
        for copy in self.copies:
            copy.wait_send()
        return total


class WeightGrads:
    def __init__(self, here, hidden, grad_in, fed, grad_fed, scratch):
        in_parts, in_got, fed_parts, fed_got, in_sems, fed_sems = scratch
        depth = in_parts.shape[1]
        product = nt(hidden[...], grad_in[...])
        for r in range(here.rows):
            in_parts[r] = product[r * depth : (r + 1) * depth].astype(BF16)
        self.first = RowSum(here, in_parts, in_got, in_sems)
        grad_now = grad_fed[...]
        for r in range(here.rows):
            fed_parts[r] = nt(grad_now, fed[r]).astype(BF16)
        self.second = RowSum(here, fed_parts, fed_got, fed_sems)

    def finish(self, in_out, fed_out):
        in_out[...] = self.first.finish()
        fed_out[...] = self.second.finish()


def scatter_sum(here, parts, near, far, near_sems, far_sems, stat=None, meanwhile=None):
    near_out, near_in = near_sems
    far_out, far_in = far_sems
    z, core = here.z, here.core
    order = list(range(1, here.zs)) + [0]
    near_copies = []
    if stat is not None:
        own, got, sums, others, stat_sems = stat
        stat_out, stat_in = stat_sems
        first = send(own, got, stat_out.at[0], stat_in.at[z], here.mate)
        first.start()
    for k in order:
        to = here.ahead(k)
        copy = send(
            parts.at[here.mate_core, to], near.at[to], near_out.at[k], near_in.at[to], here.mate
        )
        copy.start()
        near_copies.append(copy)
    far_copies = []
    if stat is not None:
        first.wait()
        sums[...] = own[...] + got[...]
        for k in range(1, here.zs):
            copy = send(
                sums, others.at[z], stat_out.at[k], stat_in.at[z], here.peer(here.ahead(k))
            )
            copy.start()
            far_copies.append(copy)
    total = None
    for i, k in enumerate(order):
        to = here.ahead(k)
        near_copies[i].wait_recv()
        both = parts[core, to].astype(F32) + near[to].astype(F32)
        if k == 0:
            total = both
        else:
            parts[core, to] = both.astype(BF16)
            copy = send(
                parts.at[core, to], far.at[z], far_out.at[k], far_in.at[z], here.peer(to)
            )
            copy.start()
            far_copies.append(copy)
    if meanwhile is not None:
        meanwhile()
    stat_total = None
    if stat is not None:
        stat_total = sums[...]
        for k in range(1, here.zs):
            src = here.behind(k)
            send(
                sums, others.at[src], stat_out.at[k], stat_in.at[src], here.peer(src)
            ).wait_recv()
            stat_total = stat_total + others[src]
    for k in range(1, here.zs):
        src = here.behind(k)
        send(
            parts.at[core, src], far.at[src], far_out.at[k], far_in.at[src], here.peer(src)
        ).wait_recv()
        total = total + far[src].astype(F32)
    for copy in near_copies:
        copy.wait_send()
    for copy in far_copies:
        copy.wait_send()
    return total, stat_total


def normalize(stream):
    average = jnp.sum(stream, 0, keepdims=True) / D
    centred = stream - average
    spread = jnp.sum(centred * centred, 0, keepdims=True) / D
    inverse = lax.rsqrt(spread + EPS)
    return centred * inverse, inverse


def gelu(u):
    inner = math.sqrt(2 / math.pi) * (u + 0.044715 * (u * u * u))
    return 0.5 * u * (1.0 + jnp.tanh(inner))


def gelu_slope(u):
    root = math.sqrt(2 / math.pi)
    t = jnp.tanh(root * (u + 0.044715 * (u * u * u)))
    return 0.5 * (1.0 + t) + 0.5 * u * (1.0 - t * t) * (root * (1.0 + 3 * 0.044715 * (u * u)))


def fed_product(here, weight, buf, kept):
    total = 0.0
    for r in range(here.rows):
        piece = flat(buf[r * here.per_row : (r + 1) * here.per_row])
        kept[r] = piece
        total = total + nn(weight[r], piece)
    return total


def attention_forward(
    sizes, stream, mod, mod_own, w_qkv, b_qkv, w_out, b_out, next_in, next_fed,
    normed, inverse, hidden, qkv, log_total, attended, branch, stream_out, all_in, all_fed,
    x_buf, a_buf, x_out, x_fwd, x_in, a_out, a_fwd, a_in, in_sems, fed_sems,
):
    here = Place(sizes)
    greet(here)
    coming = [RowGather(here, next_in, all_in, in_sems), RowGather(here, next_fed, all_fed, fed_sems)]
    x_buf[here.col] = stream[...].astype(BF16)
    gather(here, x_buf, x_out, x_fwd, x_in)
    values, inv = normalize(flat(x_buf[...]).astype(F32))
    normed[...] = values
    inverse[...] = inv
    hidden_now = (values * (1.0 + mod[:, 1:2]) + mod[:, 0:1]).astype(BF16)
    hidden[...] = hidden_now
    projected = tn(flat(w_qkv[...]), hidden_now) + b_qkv[...]
    heads = qkv.shape[0] // 3
    for i in range(3 * heads):
        qkv[i] = projected[i * HEAD : (i + 1) * HEAD].astype(BF16)
    pieces = []
    for h in range(heads):
        scores = tn(qkv[heads + h], qkv[h]) * SCALE
        highest = jnp.max(scores, axis=0, keepdims=True)
        expd = jnp.exp(scores - highest)
        summed = jnp.sum(expd, axis=0, keepdims=True)
        log_total[h] = highest + jnp.log(summed)
        probs = (expd / summed).astype(BF16)
        pieces.append(nn(qkv[2 * heads + h], probs))
    a_buf[here.col] = jnp.concatenate(pieces, axis=0).astype(BF16)
    gather(here, a_buf, a_out, a_fwd, a_in)
    branch_now = b_out[...] + fed_product(here, w_out, a_buf, attended)
    branch[...] = branch_now
    stream_out[...] = stream[...] + mod_own[:, 2:3] * branch_now
    for one in coming:
        one.finish()


def mlp_forward(sizes, more, *refs):
    stream, mod, mod_own, w_one, b_one, w_two, b_two = refs[:7]
    refs = refs[7:]
    if more:
        next_in, next_fed = refs[:2]
        refs = refs[2:]
    normed, inverse, hidden, pre, activated, branch, stream_out = refs[:7]
    refs = refs[7:]
    if more:
        all_in, all_fed = refs[:2]
        refs = refs[2:]
    x_buf, a_buf, x_out, x_fwd, x_in, a_out, a_fwd, a_in = refs[:8]
    here = Place(sizes)
    greet(here, more)
    coming = []
    if more:
        in_sems, fed_sems = refs[8:]
        coming = [RowGather(here, next_in, all_in, in_sems), RowGather(here, next_fed, all_fed, fed_sems)]
    x_buf[here.col] = stream[...].astype(BF16)
    gather(here, x_buf, x_out, x_fwd, x_in)
    values, inv = normalize(flat(x_buf[...]).astype(F32))
    normed[...] = values
    inverse[...] = inv
    hidden_now = (values * (1.0 + mod[:, 4:5]) + mod[:, 3:4]).astype(BF16)
    hidden[...] = hidden_now
    pre_now = tn(flat(w_one[...]), hidden_now) + b_one[...]
    pre[...] = pre_now
    a_buf[here.col] = gelu(pre_now).astype(BF16)
    gather(here, a_buf, a_out, a_fwd, a_in)
    branch_now = b_two[...] + fed_product(here, w_two, a_buf, activated)
    branch[...] = branch_now
    stream_out[...] = stream[...] + mod_own[:, 5:6] * branch_now
    for one in coming:
        one.finish()


def split_parts(here, parts, weight, rows):
    size = parts.shape[2]
    for r in range(here.rows):
        product = tn(weight[r], rows)
        for j in range(here.per_row):
            c = r * here.per_row + j
            parts[c % 2, c // 2] = product[j * size : (j + 1) * size].astype(BF16)


def split_norm_parts(here, parts, stat, weight, rows, normed, gain):
    size = parts.shape[2]
    product = nn(flat(weight[...]), rows)
    for c in range(here.count):
        parts[c % 2, c // 2] = product[c * size : (c + 1) * size].astype(BF16)
    scaled = product * (1.0 + gain)
    stat[...] = jnp.zeros_like(stat)
    stat[0:1] = jnp.sum(scaled, 0, keepdims=True)
    stat[1:2] = jnp.sum(scaled * normed[...], 0, keepdims=True)


def norm_back(here, grad_hidden, totals, normed, inverse, gain):
    width = grad_hidden.shape[0]
    own = normed[pl.ds(pl.multiple_of(here.col * width, 8), width)]
    scaled = grad_hidden * (1.0 + gain)
    change = inverse[...] * (scaled - totals[0:1] / D - own * (totals[1:2] / D))
    shift = jnp.sum(grad_hidden, 1, keepdims=True)
    stretch = jnp.sum(grad_hidden * own, 1, keepdims=True)
    return change, shift, stretch


def mlp_backward(sizes, more, *refs):
    grad, mod, mod_own, branch, pre, normed, inverse, w_one, w_two = refs[:9]
    refs = refs[9:]
    if more:
        feeds = refs[:4]
        refs = refs[4:]
    grad_branch, grad_pre, grad_out, sums, sums_pre = refs[:5]
    refs = refs[5:]
    if more:
        weight_outs = refs[:2]
        refs = refs[2:]
    a_parts, a_near, a_far, h_parts, h_near, h_far, stat_own, stat_got, stat_sum, stat_far = refs[:10]
    an_out, an_in, af_out, af_in, hn_out, hn_in, hf_out, hf_in, st_out, st_in = refs[10:20]
    here = Place(sizes)
    greet(here, more)
    going = []

    def meanwhile():
        if more:
            going.append(WeightGrads(here, *feeds, refs[20:]))

    grad_now = grad[...]
    grad_branch_now = (mod_own[:, 5:6] * grad_now).astype(BF16)
    grad_branch[...] = grad_branch_now
    split_parts(here, a_parts, w_two, grad_branch_now)
    grad_act, _ = scatter_sum(
        here, a_parts, a_near, a_far, (an_out, an_in), (af_out, af_in), None, meanwhile
    )
    grad_pre_now = (grad_act * gelu_slope(pre[...])).astype(BF16)
    grad_pre[...] = grad_pre_now
    split_norm_parts(here, h_parts, stat_own, w_one, grad_pre_now, normed, mod[:, 4:5])
    grad_hidden, totals = scatter_sum(
        here, h_parts, h_near, h_far, (hn_out, hn_in), (hf_out, hf_in),
        (stat_own, stat_got, stat_sum, stat_far, (st_out, st_in)),
    )
    change, shift, stretch = norm_back(
        here, grad_hidden, totals, normed, inverse, mod_own[:, 4:5]
    )
    grad_out[...] = grad_now + change
    sums[:, 0:1] = shift
    sums[:, 1:2] = stretch
    sums[:, 2:3] = jnp.sum(grad_now * branch[...], 1, keepdims=True)
    sums[:, 3:4] = jnp.sum(grad_branch_now.astype(F32), 1, keepdims=True)
    sums_pre[...] = jnp.sum(grad_pre_now.astype(F32), 1, keepdims=True)
    if more:
        going[0].finish(*weight_outs)


def attention_backward(
    sizes, grad, mod, mod_own, branch, qkv, log_total, normed, inverse, w_qkv, w_out,
    feed0, feed1, feed2, feed3,
    grad_branch, grad_qkv, grad_out, sums, sums_qkv, weight_in, weight_fed,
    a_parts, a_near, a_far, h_parts, h_near, h_far, stat_own, stat_got, stat_sum, stat_far,
    an_out, an_in, af_out, af_in, hn_out, hn_in, hf_out, hf_in, st_out, st_in, *row_scratch,
):
    here = Place(sizes)
    greet(here)
    going = []

    def meanwhile():
        going.append(WeightGrads(here, feed0, feed1, feed2, feed3, row_scratch))

    grad_now = grad[...]
    grad_branch_now = (mod_own[:, 2:3] * grad_now).astype(BF16)
    grad_branch[...] = grad_branch_now
    split_parts(here, a_parts, w_out, grad_branch_now)
    grad_att, _ = scatter_sum(
        here, a_parts, a_near, a_far, (an_out, an_in), (af_out, af_in), None, meanwhile
    )
    heads = qkv.shape[0] // 3
    queries, keys, values = [], [], []
    for h in range(heads):
        query, key, value = qkv[h], qkv[heads + h], qkv[2 * heads + h]
        grad_one = grad_att[h * HEAD : (h + 1) * HEAD].astype(BF16)
        weights = jnp.exp(tn(key, query) * SCALE - log_total[h])
        grad_weights = tn(value, grad_one)
        values.append(nt(grad_one, weights.astype(BF16)))
        inner = jnp.sum(weights * grad_weights, axis=0, keepdims=True)
        grad_scores = (weights * (grad_weights - inner)).astype(BF16)
        queries.append(nn(key, grad_scores) * SCALE)
        keys.append(nt(query, grad_scores) * SCALE)
    grad_qkv_now = jnp.concatenate(queries + keys + values, axis=0).astype(BF16)
    grad_qkv[...] = grad_qkv_now
    split_norm_parts(here, h_parts, stat_own, w_qkv, grad_qkv_now, normed, mod[:, 1:2])
    grad_hidden, totals = scatter_sum(
        here, h_parts, h_near, h_far, (hn_out, hn_in), (hf_out, hf_in),
        (stat_own, stat_got, stat_sum, stat_far, (st_out, st_in)),
    )
    change, shift, stretch = norm_back(
        here, grad_hidden, totals, normed, inverse, mod_own[:, 1:2]
    )
    grad_out[...] = grad_now + change
    sums[:, 0:1] = shift
    sums[:, 1:2] = stretch
    sums[:, 2:3] = jnp.sum(grad_now * branch[...], 1, keepdims=True)
    sums[:, 3:4] = jnp.sum(grad_branch_now.astype(F32), 1, keepdims=True)
    sums_qkv[...] = jnp.sum(grad_qkv_now.astype(F32), 1, keepdims=True)
    going[0].finish(weight_in, weight_fed)


def modulation_start(
    sizes, signal, w_mod, b_mod, next_in, next_fed,
    mod_all, signal_part, all_in, all_fed,
    sig_row, sig_col, mod_part, mod_got, mod_col,
    sig_row_sems, s_out, s_fwd, s_in, mod_sems, m_out, m_fwd, m_in, in_sems, fed_sems,
):
    here = Place(sizes)
    greet(here)
    width = signal.shape[1]
    signals = RowGather(here, signal, sig_row, sig_row_sems)
    coming = [RowGather(here, next_in, all_in, in_sems), RowGather(here, next_fed, all_fed, fed_sems)]
    signals.finish()
    sig_col[here.col] = sig_row[...].reshape(here.rows * 8, width)
    gather(here, sig_col, s_out, s_fwd, s_in)
    for j in range(here.per_row):
        signal_part[j] = sig_col[here.row * here.per_row + j]
    for i in range(LAYERS):
        product = 0.0
        for j in range(here.per_row):
            product = product + nn(
                signal_part[j].astype(BF16), w_mod[i, j * width : (j + 1) * width]
            )
        for r in range(here.rows):
            mod_part[r, i] = product[r * 8 : (r + 1) * 8]
    total = RowSum(here, mod_part, mod_got, mod_sems).finish() + b_mod[...]
    mod_col[here.col] = total
    gather(here, mod_col, m_out, m_fwd, m_in)
    mod_all[...] = mod_col[...]
    for one in coming:
        one.finish()


def modulation_end(
    sizes, grad_mod, biases, w_mod, feed0, feed1, feed2, feed3,
    mod_all, bias_sum, grad_signal, weight_in, weight_fed,
    mod_row, bias_row, back_col, back_own, back_row,
    mod_sems, bias_sems, b_out, b_fwd, b_in, back_sems, *row_scratch,
):
    here = Place(sizes)
    greet(here)
    mods = RowGather(here, grad_mod, mod_row, mod_sems)
    shares = RowGather(here, biases, bias_row, bias_sems)
    going = WeightGrads(here, feed0, feed1, feed2, feed3, row_scratch)
    mods.finish()
    mod_all[...] = mod_row[...]
    product = 0.0
    for i in range(LAYERS):
        rows = mod_row[:, i].reshape(here.rows * 8, mod_row.shape[3])
        product = product + nt(rows.astype(BF16), w_mod[i])
    back_col[here.col] = product
    gather(here, back_col, b_out, b_fwd, b_in)
    back_own[...] = jnp.sum(back_col[...], axis=0)
    backs = RowGather(here, back_own, back_row, back_sems)
    shares.finish()
    bias_sum[...] = jnp.sum(bias_row[...], axis=0)
    backs.finish()
    grad_signal[...] = back_row[
        here.col // here.per_row, pl.ds(pl.multiple_of(here.row * 8, 8), 8)
    ]
    going.finish(weight_in, weight_fed)


def run(body, ident, args, outs, scratch, far_args=0, far_outs=0):
    vmem = pl.BlockSpec(memory_space=pltpu.VMEM)
    anywhere = pl.BlockSpec(memory_space=pl.ANY)
    return pl.pallas_call(
        body,
        out_shape=[jax.ShapeDtypeStruct(shape, dtype) for shape, dtype in outs],
        in_specs=[vmem] * (len(args) - far_args) + [anywhere] * far_args,
        out_specs=[vmem] * (len(outs) - far_outs) + [anywhere] * far_outs,
        scratch_shapes=scratch,
        compiler_params=pltpu.CompilerParams(
            collective_id=ident, has_side_effects=True, vmem_limit_bytes=VMEM_BYTES
        ),
    )(*args)


def dma(*shape):
    return pltpu.SemaphoreType.DMA(shape)


def gather_scratch(count, sizes, width):
    bufs = [pltpu.VMEM((count, size, width), BF16) for size in sizes]
    return bufs + [dma(count) for _ in range(3 * len(sizes))]


def scatter_scratch(count, sizes, width):
    zs = count // 2
    bufs = []
    for size in sizes:
        bufs.append(pltpu.VMEM((2, zs, size, width), BF16))
        bufs.append(pltpu.VMEM((zs, size, width), BF16))
        bufs.append(pltpu.VMEM((zs, size, width), BF16))
    bufs += [pltpu.VMEM((8, width), F32) for _ in range(3)]
    bufs.append(pltpu.VMEM((zs, 8, width), F32))
    return bufs + [dma(zs) for _ in range(4 * len(sizes) + 2)]


def per_device(
    sizes,
    tokens, cond, w_mod, b_mod, query_key_value_weight, b_qv,
    attention_output_weight, attention_output_bias, first_linear_weight, first_linear_bias,
    second_linear_weight, second_linear_bias, cotangent,
):
    rows, count = sizes
    assert cond.shape[0] == 1
    length, width = tokens.shape
    heads = width // HEAD
    hidden_width = first_linear_weight.shape[2]
    rows_in = w_mod.shape[1]
    rows_fed = second_linear_weight.shape[1]
    per_row = count // rows
    cond_float = cond.astype(F32)
    signal = jax.nn.silu(cond_float).astype(BF16).astype(F32)
    w_mod_flat = w_mod.reshape(LAYERS, rows_in, 6 * width)

    shards = []
    for i in range(LAYERS):
        shards.append(
            (
                query_key_value_weight[i].reshape(rows_in, 3 * width),
                attention_output_weight[i].T,
                first_linear_weight[i],
                second_linear_weight[i].T,
            )
        )

    def gathered(first):
        if first:
            return [((rows, rows_in, 3 * width), BF16), ((rows, width, rows_in), BF16)]
        return [((rows, rows_in, hidden_width), BF16), ((rows, width, rows_fed), BF16)]

    def grads(first):
        return [(shape[1:], F32) for shape, _ in gathered(first)]

    def grad_scratch(first):
        (one, _), (two, _) = gathered(first)
        return [
            pltpu.VMEM(one, BF16),
            pltpu.VMEM(one, BF16),
            pltpu.VMEM(two, BF16),
            pltpu.VMEM(two, BF16),
            dma(2, rows),
            dma(2, rows),
        ]

    mod_all, signal_part, w_qkv, w_out = run(
        functools.partial(modulation_start, sizes), 0,
        (
            jnp.broadcast_to(signal, (8, width)),
            w_mod_flat,
            b_mod.reshape(LAYERS, 1, 6 * width),
            shards[0][0],
            shards[0][1],
        ),
        [
            ((count, LAYERS, 8, 6 * width), F32),
            ((per_row, rows * 8, width), F32),
        ]
        + gathered(True),
        [
            pltpu.VMEM((rows, 8, width), F32),
            pltpu.VMEM((count, rows * 8, width), F32),
            pltpu.VMEM((rows, LAYERS, 8, 6 * width), F32),
            pltpu.VMEM((rows, LAYERS, 8, 6 * width), F32),
            pltpu.VMEM((count, LAYERS, 8, 6 * width), F32),
            dma(2, rows), dma(count), dma(count), dma(count),
            dma(2, rows), dma(count), dma(count), dma(count),
            dma(2, rows), dma(2, rows),
        ],
        2, 2,
    )
    mods = mod_all[:, :, 0].reshape(count, LAYERS, 6, width).transpose(1, 0, 3, 2)
    mod_full = mods.reshape(LAYERS, D, 6)
    mod_own = lax.dynamic_index_in_dim(mods, lax.axis_index("col"), 1, keepdims=False)

    stream = tokens.astype(F32).T
    saved = []
    for i in range(LAYERS):
        bias = jnp.concatenate([b_qv[i, 0], jnp.zeros_like(b_qv[i, 0]), b_qv[i, 1]])[:, None]
        normed1, inverse1, hidden1, qkv, log_total, attended, branch1, stream, w_one, w_two = run(
            functools.partial(attention_forward, sizes), 1,
            (
                stream, mod_full[i], mod_own[i], w_qkv, bias, w_out,
                attention_output_bias[i][:, None], shards[i][2], shards[i][3],
            ),
            [
                ((D, length), F32),
                ((1, length), F32),
                ((D, length), BF16),
                ((3 * heads, HEAD, length), BF16),
                ((heads, 1, length), F32),
                ((rows, rows_in, length), BF16),
                ((width, length), F32),
                ((width, length), F32),
            ]
            + gathered(False),
            gather_scratch(count, (width, width), length) + [dma(2, rows), dma(2, rows)],
            2, 2,
        )
        more = i + 1 < LAYERS
        results = run(
            functools.partial(mlp_forward, sizes, more), 2 if more else 3,
            (
                stream, mod_full[i], mod_own[i], w_one, first_linear_bias[i][:, None], w_two,
                second_linear_bias[i][:, None],
            )
            + (shards[i + 1][:2] if more else ()),
            [
                ((D, length), F32),
                ((1, length), F32),
                ((D, length), BF16),
                ((hidden_width, length), F32),
                ((rows, rows_fed, length), BF16),
                ((width, length), F32),
                ((width, length), F32),
            ]
            + (gathered(True) if more else []),
            gather_scratch(count, (width, hidden_width), length)
            + ([dma(2, rows), dma(2, rows)] if more else []),
            2 if more else 0, 2 if more else 0,
        )
        normed2, inverse2, hidden2, pre, activated, branch2, stream = results[:7]
        saved.append(
            (
                normed1, inverse1, hidden1, qkv, log_total, attended, branch1,
                normed2, inverse2, hidden2, pre, activated, branch2,
                w_qkv, w_out, w_one, w_two,
            )
        )
        if more:
            w_qkv, w_out = results[7:]
    output = stream.T.astype(BF16)

    grad = cotangent.astype(F32).T
    grad_mods = [None] * LAYERS
    biases = [None] * LAYERS
    first_grads = [None] * LAYERS
    second_grads = [None] * LAYERS
    waiting = None
    for i in reversed(range(LAYERS)):
        (
            normed1, inverse1, hidden1, qkv, log_total, attended, branch1,
            normed2, inverse2, hidden2, pre, activated, branch2,
            w_qkv, w_out, w_one, w_two,
        ) = saved[i]
        more = waiting is not None
        results = run(
            functools.partial(mlp_backward, sizes, more), 6 if more else 4,
            (grad, mod_full[i], mod_own[i], branch2, pre, normed2, inverse2, w_one, w_two)
            + (waiting if more else ()),
            [
                ((width, length), BF16),
                ((hidden_width, length), BF16),
                ((width, length), F32),
                ((width, 4), F32),
                ((hidden_width, 1), F32),
            ]
            + (grads(True) if more else []),
            scatter_scratch(count, (hidden_width, width), length)
            + (grad_scratch(True) if more else []),
        )
        grad_branch2, grad_pre, grad, sums2, sums_pre = results[:5]
        if more:
            first_grads[i + 1] = results[5:]
        grad_branch1, grad_qkv, grad, sums1, sums_qkv, *second_grads[i] = run(
            functools.partial(attention_backward, sizes), 5,
            (
                grad, mod_full[i], mod_own[i], branch1, qkv, log_total, normed1, inverse1,
                w_qkv, w_out, hidden2, grad_pre, activated, grad_branch2,
            ),
            [
                ((width, length), BF16),
                ((3 * width, length), BF16),
                ((width, length), F32),
                ((width, 4), F32),
                ((3 * width, 1), F32),
            ]
            + grads(False),
            scatter_scratch(count, (width, width), length) + grad_scratch(False),
        )
        waiting = (hidden1, grad_qkv, attended, grad_branch1)
        grad_mods[i] = jnp.concatenate([sums1[:, 0:3], sums2[:, 0:3]], axis=1).T.astype(BF16)
        biases[i] = jnp.concatenate(
            [sums_qkv[:width, 0], sums_qkv[2 * width :, 0], sums1[:, 3], sums2[:, 3], sums_pre[:, 0]]
        )
    mod_grad = jnp.stack(grad_mods).reshape(LAYERS, 1, 6 * width).astype(F32)
    bias_grad = jnp.stack(biases).reshape(1, -1)
    mod_grad_all, bias_sum, grad_signal, *first_grads[0] = run(
        functools.partial(modulation_end, sizes), 7,
        (
            jnp.broadcast_to(mod_grad, (LAYERS, 8, 6 * width)),
            jnp.broadcast_to(bias_grad, (8, bias_grad.shape[1])),
            w_mod_flat,
        )
        + waiting,
        [
            ((rows, LAYERS, 8, 6 * width), F32),
            ((8, bias_grad.shape[1]), F32),
            ((8, rows_in), F32),
        ]
        + grads(True),
        [
            pltpu.VMEM((rows, LAYERS, 8, 6 * width), F32),
            pltpu.VMEM((rows, 8, bias_grad.shape[1]), F32),
            pltpu.VMEM((count, rows * 8, rows_in), F32),
            pltpu.VMEM((rows * 8, rows_in), F32),
            pltpu.VMEM((rows, rows * 8, rows_in), F32),
            dma(2, rows), dma(2, rows), dma(count), dma(count), dma(count), dma(2, rows),
        ]
        + grad_scratch(True),
    )
    signals = signal_part.reshape(per_row, rows, 8, width)[:, :, 0]
    signals = signals.transpose(1, 0, 2).reshape(rows, rows_in)
    mod_rows = mod_grad_all[:, :, 0]
    grad_w_mod = jnp.einsum(
        "ri,rlj->lij",
        signals.astype(BF16),
        mod_rows.astype(BF16),
        preferred_element_type=F32,
    ).reshape(LAYERS, rows_in, 6, width)
    grad_b_mod = jnp.sum(mod_rows, 0).reshape(LAYERS, 6, width)
    grad_signal = lax.dynamic_slice(
        grad_signal[:1], (0, lax.axis_index("col") % per_row * width), (1, width)
    )
    grad_cond = jax.vjp(jax.nn.silu, cond_float)[1](grad_signal)[0]
    bias_sum = bias_sum[0].reshape(LAYERS, -1)
    return (
        output,
        grad.T,
        grad_cond,
        grad_w_mod,
        grad_b_mod,
        jnp.stack([one[0] for one in first_grads]).reshape(LAYERS, rows_in, 3, width),
        bias_sum[:, : 2 * width].reshape(LAYERS, 2, width),
        jnp.stack([one[1].T for one in first_grads]),
        bias_sum[:, 2 * width : 3 * width],
        jnp.stack([one[0] for one in second_grads]),
        bias_sum[:, 4 * width :],
        jnp.stack([one[1].T for one in second_grads]),
        bias_sum[:, 3 * width : 4 * width],
    )


def solution(mesh):
    in_specs = (
        P("row", "col"),
        P("row", "col"),
        P(None, "row", None, "col"),
        P(None, None, "col"),
        P(None, "row", None, "col"),
        P(None, None, "col"),
        P(None, "row", "col"),
        P(None, "col"),
        P(None, "row", "col"),
        P(None, "col"),
        P(None, "row", "col"),
        P(None, "col"),
        P("row", "col"),
    )
    out_specs = (
        P("row", "col"),
        P("row", "col"),
        P("row", "col"),
        P(None, "row", None, "col"),
        P(None, None, "col"),
        P(None, "row", None, "col"),
        P(None, None, "col"),
        P(None, "row", "col"),
        P(None, "col"),
        P(None, "row", "col"),
        P(None, "col"),
        P(None, "row", "col"),
        P(None, "col"),
    )
    return jax.shard_map(
        functools.partial(per_device, (mesh.shape["row"], mesh.shape["col"])),
        mesh=mesh,
        in_specs=in_specs,
        out_specs=out_specs,
        check_vma=False,
    )
```

```python
import functools
import math

import jax
import jax.numpy as jnp
from jax import lax
from jax.experimental import pallas as pl
from jax.experimental.pallas import tpu as pltpu
from jax.sharding import PartitionSpec as P

D = 1152
HEAD = 72
LAYERS = 2
EPS = 1e-06
SCALE = HEAD ** (-0.5)
BF16 = jnp.bfloat16
F32 = jnp.float32
MESH = pl.DeviceIdType.MESH
VMEM_BYTES = 52 * 1024 * 1024


def nn(a, b):
    return lax.dot_general(a, b, (((1,), (0,)), ((), ())), preferred_element_type=F32)


def tn(a, b):
    return lax.dot_general(a, b, (((0,), (0,)), ((), ())), preferred_element_type=F32)


def nt(a, b):
    return lax.dot_general(a, b, (((1,), (1,)), ((), ())), preferred_element_type=F32)


def flat(x):
    blocks, rows, columns = x.shape
    if rows % 16 == 0:
        return x.reshape(blocks * rows, columns)
    return x.astype(F32).reshape(blocks * rows, columns).astype(x.dtype)


class Place:
    def __init__(self, sizes):
        rows, count = sizes
        self.rows = rows
        self.per_row = count // rows
        self.row = lax.axis_index("row")
        self.col = lax.axis_index("col")
        self.count = count
        self.zs = count // 2
        self.z = self.col // 2
        self.core = self.col % 2
        self.mate_core = 1 - self.core
        self.mate = (self.row, self.z * 2 + self.mate_core)

    def ahead(self, k):
        return lax.rem(self.z + k, self.zs)

    def behind(self, k):
        return lax.rem(self.z + self.zs - k, self.zs)

    def peer(self, z):
        return (self.row, z * 2 + self.core)

    def below(self, k):
        return lax.rem(self.row + k, self.rows)

    def above(self, k):
        return lax.rem(self.row + self.rows - k, self.rows)


def greet(here, with_rows=True):
    barrier = pltpu.get_barrier_semaphore()
    pl.semaphore_signal(barrier, inc=1, device_id=here.mate, device_id_type=MESH)
    for k in range(1, here.zs):
        pl.semaphore_signal(
            barrier, inc=1, device_id=here.peer(here.ahead(k)), device_id_type=MESH
        )
    if with_rows:
        for k in range(1, here.rows):
            pl.semaphore_signal(
                barrier, inc=1, device_id=(here.below(k), here.col), device_id_type=MESH
            )
        pl.semaphore_wait(barrier, here.zs + here.rows - 1)
    else:
        pl.semaphore_wait(barrier, here.zs)


def send(src, dst, send_sem, recv_sem, device):
    return pltpu.make_async_remote_copy(
        src_ref=src,
        dst_ref=dst,
        send_sem=send_sem,
        recv_sem=recv_sem,
        device_id=device,
        device_id_type=MESH,
    )


def gather(here, buf, out_sem, fwd_sem, in_sem):
    own = here.col
    started = []
    for k in range(1, here.zs):
        copy = send(
            buf.at[own], buf.at[own], out_sem.at[k], in_sem.at[own], here.peer(here.ahead(k))
        )
        copy.start()
        started.append(copy)
    copy = send(buf.at[own], buf.at[own], out_sem.at[0], in_sem.at[own], here.mate)
    copy.start()
    started.append(copy)
    for k in range(1, here.zs):
        src = here.behind(k) * 2 + here.core
        copy = send(buf.at[src], buf.at[src], fwd_sem.at[k], in_sem.at[src], here.mate)
        copy.wait_recv()
        copy.start()
        started.append(copy)
    for k in range(here.zs):
        src = here.behind(k) * 2 + here.mate_core
        send(buf.at[src], buf.at[src], fwd_sem.at[0], in_sem.at[src], here.mate).wait_recv()
    for copy in started:
        copy.wait_send()


class RowGather:
    def __init__(self, here, src, dst, sems):
        self.here, self.src, self.dst = here, src, dst
        self.out, self.into = sems.at[0], sems.at[1]
        own = here.row
        self.local = pltpu.make_async_copy(src, dst.at[own], self.out.at[0])
        self.local.start()
        self.copies = []
        for k in range(1, here.rows):
            copy = send(
                src, dst.at[own], self.out.at[k], self.into.at[own], (here.below(k), here.col)
            )
            copy.start()
            self.copies.append(copy)

    def finish(self):
        here = self.here
        self.local.wait()
        for k in range(1, here.rows):
            src = here.above(k)
            send(
                self.src, self.dst.at[src], self.out.at[k], self.into.at[src], (src, here.col)
            ).wait_recv()
        for copy in self.copies:
            copy.wait_send()


class RowSum:
    def __init__(self, here, parts, got, sems):
        self.here, self.parts, self.got = here, parts, got
        self.out, self.into = sems.at[0], sems.at[1]
        self.copies = []
        for k in range(1, here.rows):
            to = here.below(k)
            copy = send(
                parts.at[to],
                got.at[here.row],
                self.out.at[k],
                self.into.at[here.row],
                (to, here.col),
            )
            copy.start()
            self.copies.append(copy)

    def finish(self):
        here = self.here
        total = self.parts[here.row].astype(F32)
        for k in range(1, here.rows):
            src = here.above(k)
            send(
                self.parts.at[src],
                self.got.at[src],
                self.out.at[k],
                self.into.at[src],
                (src, here.col),
            ).wait_recv()
            total = total + self.got[src].astype(F32)
        for copy in self.copies:
            copy.wait_send()
        return total


def in_grad(here, hidden, grad, scratch):
    parts, got, sems = scratch
    depth = parts.shape[1]
    product = nt(hidden[...], grad[...])
    for r in range(here.rows):
        parts[r] = product[r * depth : (r + 1) * depth].astype(BF16)
    return RowSum(here, parts, got, sems)


def fed_grad(here, fed, grad, scratch):
    parts, got, sems = scratch
    grad_now = grad[...]
    for r in range(here.rows):
        parts[r] = nt(grad_now, fed[r]).astype(BF16)
    return RowSum(here, parts, got, sems)


def scatter_sum(here, parts, near, far, near_sems, far_sems, stat=None, meanwhile=None):
    near_out, near_in = near_sems
    far_out, far_in = far_sems
    z, core = here.z, here.core
    order = list(range(1, here.zs)) + [0]
    near_copies = []
    if stat is not None:
        own, got, sums, others, stat_sems = stat
        stat_out, stat_in = stat_sems
        first = send(own, got, stat_out.at[0], stat_in.at[z], here.mate)
        first.start()
    for k in order:
        to = here.ahead(k)
        copy = send(
            parts.at[here.mate_core, to], near.at[to], near_out.at[k], near_in.at[to], here.mate
        )
        copy.start()
        near_copies.append(copy)
    far_copies = []
    if stat is not None:
        first.wait()
        sums[...] = own[...] + got[...]
        for k in range(1, here.zs):
            copy = send(
                sums, others.at[z], stat_out.at[k], stat_in.at[z], here.peer(here.ahead(k))
            )
            copy.start()
            far_copies.append(copy)
    total = None
    for i, k in enumerate(order):
        to = here.ahead(k)
        near_copies[i].wait_recv()
        both = parts[core, to].astype(F32) + near[to].astype(F32)
        if k == 0:
            total = both
        else:
            parts[core, to] = both.astype(BF16)
            copy = send(
                parts.at[core, to], far.at[z], far_out.at[k], far_in.at[z], here.peer(to)
            )
            copy.start()
            far_copies.append(copy)
    if meanwhile is not None:
        meanwhile()
    stat_total = None
    if stat is not None:
        stat_total = sums[...]
        for k in range(1, here.zs):
            src = here.behind(k)
            send(
                sums, others.at[src], stat_out.at[k], stat_in.at[src], here.peer(src)
            ).wait_recv()
            stat_total = stat_total + others[src]
    for k in range(1, here.zs):
        src = here.behind(k)
        send(
            parts.at[core, src], far.at[src], far_out.at[k], far_in.at[src], here.peer(src)
        ).wait_recv()
        total = total + far[src].astype(F32)
    for copy in near_copies:
        copy.wait_send()
    for copy in far_copies:
        copy.wait_send()
    return total, stat_total


def normalize(stream):
    average = jnp.sum(stream, 0, keepdims=True) / D
    centred = stream - average
    spread = jnp.sum(centred * centred, 0, keepdims=True) / D
    inverse = lax.rsqrt(spread + EPS)
    return centred * inverse, inverse


def gelu(u):
    inner = math.sqrt(2 / math.pi) * (u + 0.044715 * (u * u * u))
    return 0.5 * u * (1.0 + jnp.tanh(inner))


def gelu_slope(u):
    root = math.sqrt(2 / math.pi)
    t = jnp.tanh(root * (u + 0.044715 * (u * u * u)))
    return 0.5 * (1.0 + t) + 0.5 * u * (1.0 - t * t) * (root * (1.0 + 3 * 0.044715 * (u * u)))


def fed_product(here, weight, buf, kept):
    total = 0.0
    for r in range(here.rows):
        piece = flat(buf[r * here.per_row : (r + 1) * here.per_row])
        kept[r] = piece
        total = total + nn(weight[r], piece)
    return total


def attention_forward(
    sizes, stream, mod, mod_own, w_qkv, b_qkv, b_out, fed, next_in,
    normed, inverse, hidden, qkv, log_total, attended, branch, stream_out, w_out, all_in,
    x_buf, a_buf, x_out, x_fwd, x_in, a_out, a_fwd, a_in, w_buf, fed_sems, in_sems,
):
    here = Place(sizes)
    greet(here)
    needed = RowGather(here, fed, w_buf, fed_sems)
    coming = RowGather(here, next_in, all_in, in_sems)
    x_buf[here.col] = stream[...].astype(BF16)
    gather(here, x_buf, x_out, x_fwd, x_in)
    values, inv = normalize(flat(x_buf[...]).astype(F32))
    normed[...] = values
    inverse[...] = inv
    hidden_now = (values * (1.0 + mod[:, 1:2]) + mod[:, 0:1]).astype(BF16)
    hidden[...] = hidden_now
    projected = tn(flat(w_qkv[...]), hidden_now) + b_qkv[...]
    heads = qkv.shape[0] // 3
    for i in range(3 * heads):
        qkv[i] = projected[i * HEAD : (i + 1) * HEAD].astype(BF16)
    pieces = []
    for h in range(heads):
        scores = tn(qkv[heads + h], qkv[h]) * SCALE
        highest = jnp.max(scores, axis=0, keepdims=True)
        expd = jnp.exp(scores - highest)
        summed = jnp.sum(expd, axis=0, keepdims=True)
        log_total[h] = highest + jnp.log(summed)
        probs = (expd / summed).astype(BF16)
        pieces.append(nn(qkv[2 * heads + h], probs))
    a_buf[here.col] = jnp.concatenate(pieces, axis=0).astype(BF16)
    gather(here, a_buf, a_out, a_fwd, a_in)
    needed.finish()
    w_out[...] = w_buf[...]
    branch_now = b_out[...] + fed_product(here, w_buf, a_buf, attended)
    branch[...] = branch_now
    stream_out[...] = stream[...] + mod_own[:, 2:3] * branch_now
    coming.finish()


def mlp_forward(sizes, more, *refs):
    stream, mod, mod_own, w_one, b_one, b_two, fed = refs[:7]
    refs = refs[7:]
    if more:
        next_in = refs[0]
        refs = refs[1:]
    normed, inverse, hidden, pre, activated, branch, stream_out, w_two = refs[:8]
    refs = refs[8:]
    if more:
        all_in = refs[0]
        refs = refs[1:]
    x_buf, a_buf, x_out, x_fwd, x_in, a_out, a_fwd, a_in, w_buf, fed_sems = refs[:10]
    here = Place(sizes)
    greet(here)
    needed = RowGather(here, fed, w_buf, fed_sems)
    if more:
        coming = RowGather(here, next_in, all_in, refs[10])
    x_buf[here.col] = stream[...].astype(BF16)
    gather(here, x_buf, x_out, x_fwd, x_in)
    values, inv = normalize(flat(x_buf[...]).astype(F32))
    normed[...] = values
    inverse[...] = inv
    hidden_now = (values * (1.0 + mod[:, 4:5]) + mod[:, 3:4]).astype(BF16)
    hidden[...] = hidden_now
    pre_now = tn(flat(w_one[...]), hidden_now) + b_one[...]
    pre[...] = pre_now
    a_buf[here.col] = gelu(pre_now).astype(BF16)
    gather(here, a_buf, a_out, a_fwd, a_in)
    needed.finish()
    w_two[...] = w_buf[...]
    branch_now = b_two[...] + fed_product(here, w_buf, a_buf, activated)
    branch[...] = branch_now
    stream_out[...] = stream[...] + mod_own[:, 5:6] * branch_now
    if more:
        coming.finish()


def split_parts(here, parts, weight, rows):
    size = parts.shape[2]
    for r in range(here.rows):
        product = tn(weight[r], rows)
        for j in range(here.per_row):
            c = r * here.per_row + j
            parts[c % 2, c // 2] = product[j * size : (j + 1) * size].astype(BF16)


def split_norm_parts(here, parts, stat, weight, rows, normed, gain):
    size = parts.shape[2]
    product = nn(flat(weight[...]), rows)
    for c in range(here.count):
        parts[c % 2, c // 2] = product[c * size : (c + 1) * size].astype(BF16)
    scaled = product * (1.0 + gain)
    stat[...] = jnp.zeros_like(stat)
    stat[0:1] = jnp.sum(scaled, 0, keepdims=True)
    stat[1:2] = jnp.sum(scaled * normed[...], 0, keepdims=True)


def norm_back(here, grad_hidden, totals, normed, inverse, gain):
    width = grad_hidden.shape[0]
    own = normed[pl.ds(pl.multiple_of(here.col * width, 8), width)]
    scaled = grad_hidden * (1.0 + gain)
    change = inverse[...] * (scaled - totals[0:1] / D - own * (totals[1:2] / D))
    shift = jnp.sum(grad_hidden, 1, keepdims=True)
    stretch = jnp.sum(grad_hidden * own, 1, keepdims=True)
    return change, shift, stretch


def mlp_backward(sizes, more, *refs):
    grad, mod, mod_own, branch, pre, normed, inverse, w_one, w_two, activated = refs[:10]
    refs = refs[10:]
    if more:
        feeds = refs[:2]
        refs = refs[2:]
    grad_branch, grad_pre, grad_out, sums, sums_pre, weight_fed = refs[:6]
    refs = refs[6:]
    if more:
        weight_in = refs[0]
        refs = refs[1:]
    a_parts, a_near, a_far, h_parts, h_near, h_far, stat_own, stat_got, stat_sum, stat_far = refs[:10]
    an_out, an_in, af_out, af_in, hn_out, hn_in, hf_out, hf_in, st_out, st_in = refs[10:20]
    here = Place(sizes)
    greet(here)
    going = []

    def meanwhile():
        going.append(fed_grad(here, activated, grad_branch, refs[20:23]))
        if more:
            going.append(in_grad(here, *feeds, refs[23:26]))

    grad_now = grad[...]
    grad_branch_now = (mod_own[:, 5:6] * grad_now).astype(BF16)
    grad_branch[...] = grad_branch_now
    split_parts(here, a_parts, w_two, grad_branch_now)
    grad_act, _ = scatter_sum(
        here, a_parts, a_near, a_far, (an_out, an_in), (af_out, af_in), None, meanwhile
    )
    grad_pre_now = (grad_act * gelu_slope(pre[...])).astype(BF16)
    grad_pre[...] = grad_pre_now
    split_norm_parts(here, h_parts, stat_own, w_one, grad_pre_now, normed, mod[:, 4:5])
    grad_hidden, totals = scatter_sum(
        here, h_parts, h_near, h_far, (hn_out, hn_in), (hf_out, hf_in),
        (stat_own, stat_got, stat_sum, stat_far, (st_out, st_in)),
    )
    change, shift, stretch = norm_back(
        here, grad_hidden, totals, normed, inverse, mod_own[:, 4:5]
    )
    grad_out[...] = grad_now + change
    sums[:, 0:1] = shift
    sums[:, 1:2] = stretch
    sums[:, 2:3] = jnp.sum(grad_now * branch[...], 1, keepdims=True)
    sums[:, 3:4] = jnp.sum(grad_branch_now.astype(F32), 1, keepdims=True)
    sums_pre[...] = jnp.sum(grad_pre_now.astype(F32), 1, keepdims=True)
    weight_fed[...] = going[0].finish()
    if more:
        weight_in[...] = going[1].finish()


def attention_backward(
    sizes, grad, mod, mod_own, branch, qkv, log_total, normed, inverse, w_qkv, w_out,
    attended, hidden_two, grad_pre,
    grad_branch, grad_qkv, grad_out, sums, sums_qkv, weight_fed, weight_in,
    a_parts, a_near, a_far, h_parts, h_near, h_far, stat_own, stat_got, stat_sum, stat_far,
    an_out, an_in, af_out, af_in, hn_out, hn_in, hf_out, hf_in, st_out, st_in, *row_scratch,
):
    here = Place(sizes)
    greet(here)
    going = []

    def meanwhile():
        going.append(fed_grad(here, attended, grad_branch, row_scratch[:3]))
        going.append(in_grad(here, hidden_two, grad_pre, row_scratch[3:]))

    grad_now = grad[...]
    grad_branch_now = (mod_own[:, 2:3] * grad_now).astype(BF16)
    grad_branch[...] = grad_branch_now
    split_parts(here, a_parts, w_out, grad_branch_now)
    grad_att, _ = scatter_sum(
        here, a_parts, a_near, a_far, (an_out, an_in), (af_out, af_in), None, meanwhile
    )
    heads = qkv.shape[0] // 3
    queries, keys, values = [], [], []
    for h in range(heads):
        query, key, value = qkv[h], qkv[heads + h], qkv[2 * heads + h]
        grad_one = grad_att[h * HEAD : (h + 1) * HEAD].astype(BF16)
        weights = jnp.exp(tn(key, query) * SCALE - log_total[h])
        grad_weights = tn(value, grad_one)
        values.append(nt(grad_one, weights.astype(BF16)))
        inner = jnp.sum(weights * grad_weights, axis=0, keepdims=True)
        grad_scores = (weights * (grad_weights - inner)).astype(BF16)
        queries.append(nn(key, grad_scores) * SCALE)
        keys.append(nt(query, grad_scores) * SCALE)
    grad_qkv_now = jnp.concatenate(queries + keys + values, axis=0).astype(BF16)
    grad_qkv[...] = grad_qkv_now
    split_norm_parts(here, h_parts, stat_own, w_qkv, grad_qkv_now, normed, mod[:, 1:2])
    grad_hidden, totals = scatter_sum(
        here, h_parts, h_near, h_far, (hn_out, hn_in), (hf_out, hf_in),
        (stat_own, stat_got, stat_sum, stat_far, (st_out, st_in)),
    )
    change, shift, stretch = norm_back(
        here, grad_hidden, totals, normed, inverse, mod_own[:, 1:2]
    )
    grad_out[...] = grad_now + change
    sums[:, 0:1] = shift
    sums[:, 1:2] = stretch
    sums[:, 2:3] = jnp.sum(grad_now * branch[...], 1, keepdims=True)
    sums[:, 3:4] = jnp.sum(grad_branch_now.astype(F32), 1, keepdims=True)
    sums_qkv[...] = jnp.sum(grad_qkv_now.astype(F32), 1, keepdims=True)
    weight_fed[...] = going[0].finish()
    weight_in[...] = going[1].finish()


def modulation_start(
    sizes, signal, w_mod, b_mod, next_in,
    mod_all, signal_part, all_in,
    sig_row, sig_col, mod_part, mod_got, mod_col,
    sig_row_sems, s_out, s_fwd, s_in, mod_sems, m_out, m_fwd, m_in, in_sems,
):
    here = Place(sizes)
    greet(here)
    width = signal.shape[1]
    signals = RowGather(here, signal, sig_row, sig_row_sems)
    coming = RowGather(here, next_in, all_in, in_sems)
    signals.finish()
    sig_col[here.col] = sig_row[...].reshape(here.rows * 8, width)
    gather(here, sig_col, s_out, s_fwd, s_in)
    for j in range(here.per_row):
        signal_part[j] = sig_col[here.row * here.per_row + j]
    for i in range(LAYERS):
        product = 0.0
        for j in range(here.per_row):
            product = product + nn(
                signal_part[j].astype(BF16), w_mod[i, j * width : (j + 1) * width]
            )
        for r in range(here.rows):
            mod_part[r, i] = product[r * 8 : (r + 1) * 8]
    total = RowSum(here, mod_part, mod_got, mod_sems).finish() + b_mod[...]
    mod_col[here.col] = total
    gather(here, mod_col, m_out, m_fwd, m_in)
    mod_all[...] = mod_col[...]
    coming.finish()


def modulation_end(
    sizes, grad_mod, biases, w_mod, hidden, grad_qkv,
    mod_all, bias_sum, grad_signal, weight_in,
    mod_row, bias_row, back_col, back_own, back_row,
    mod_sems, bias_sems, b_out, b_fwd, b_in, back_sems, *row_scratch,
):
    here = Place(sizes)
    greet(here)
    mods = RowGather(here, grad_mod, mod_row, mod_sems)
    shares = RowGather(here, biases, bias_row, bias_sems)
    going = in_grad(here, hidden, grad_qkv, row_scratch)
    mods.finish()
    mod_all[...] = mod_row[...]
    product = 0.0
    for i in range(LAYERS):
        rows = mod_row[:, i].reshape(here.rows * 8, mod_row.shape[3])
        product = product + nt(rows.astype(BF16), w_mod[i])
    back_col[here.col] = product
    gather(here, back_col, b_out, b_fwd, b_in)
    back_own[...] = jnp.sum(back_col[...], axis=0)
    backs = RowGather(here, back_own, back_row, back_sems)
    shares.finish()
    bias_sum[...] = jnp.sum(bias_row[...], axis=0)
    backs.finish()
    grad_signal[...] = back_row[
        here.col // here.per_row, pl.ds(pl.multiple_of(here.row * 8, 8), 8)
    ]
    weight_in[...] = going.finish()


def run(body, ident, args, outs, scratch, far_args=0, far_outs=0):
    vmem = pl.BlockSpec(memory_space=pltpu.VMEM)
    anywhere = pl.BlockSpec(memory_space=pl.ANY)
    return pl.pallas_call(
        body,
        out_shape=[jax.ShapeDtypeStruct(shape, dtype) for shape, dtype in outs],
        in_specs=[vmem] * (len(args) - far_args) + [anywhere] * far_args,
        out_specs=[vmem] * (len(outs) - far_outs) + [anywhere] * far_outs,
        scratch_shapes=scratch,
        compiler_params=pltpu.CompilerParams(
            collective_id=ident, has_side_effects=True, vmem_limit_bytes=VMEM_BYTES
        ),
    )(*args)


def dma(*shape):
    return pltpu.SemaphoreType.DMA(shape)


def gather_scratch(count, sizes, width):
    bufs = [pltpu.VMEM((count, size, width), BF16) for size in sizes]
    return bufs + [dma(count) for _ in range(3 * len(sizes))]


def scatter_scratch(count, sizes, width):
    zs = count // 2
    bufs = []
    for size in sizes:
        bufs.append(pltpu.VMEM((2, zs, size, width), BF16))
        bufs.append(pltpu.VMEM((zs, size, width), BF16))
        bufs.append(pltpu.VMEM((zs, size, width), BF16))
    bufs += [pltpu.VMEM((8, width), F32) for _ in range(3)]
    bufs.append(pltpu.VMEM((zs, 8, width), F32))
    return bufs + [dma(zs) for _ in range(4 * len(sizes) + 2)]


def per_device(
    sizes,
    tokens, cond, w_mod, b_mod, query_key_value_weight, b_qv,
    attention_output_weight, attention_output_bias, first_linear_weight, first_linear_bias,
    second_linear_weight, second_linear_bias, cotangent,
):
    rows, count = sizes
    assert cond.shape[0] == 1
    length, width = tokens.shape
    heads = width // HEAD
    hidden_width = first_linear_weight.shape[2]
    rows_in = w_mod.shape[1]
    rows_fed = second_linear_weight.shape[1]
    per_row = count // rows
    cond_float = cond.astype(F32)
    signal = jax.nn.silu(cond_float).astype(BF16).astype(F32)
    w_mod_flat = w_mod.reshape(LAYERS, rows_in, 6 * width)

    shards = []
    for i in range(LAYERS):
        shards.append(
            (
                query_key_value_weight[i].reshape(rows_in, 3 * width),
                attention_output_weight[i].T,
                first_linear_weight[i],
                second_linear_weight[i].T,
            )
        )

    shape_qkv = (rows, rows_in, 3 * width)
    shape_out = (rows, width, rows_in)
    shape_one = (rows, rows_in, hidden_width)
    shape_two = (rows, width, rows_fed)

    def sum_scratch(*shapes):
        scratch = []
        for shape in shapes:
            scratch += [pltpu.VMEM(shape, BF16), pltpu.VMEM(shape, BF16), dma(2, rows)]
        return scratch

    mod_all, signal_part, w_qkv = run(
        functools.partial(modulation_start, sizes), 0,
        (
            jnp.broadcast_to(signal, (8, width)),
            w_mod_flat,
            b_mod.reshape(LAYERS, 1, 6 * width),
            shards[0][0],
        ),
        [
            ((count, LAYERS, 8, 6 * width), F32),
            ((per_row, rows * 8, width), F32),
            (shape_qkv, BF16),
        ],
        [
            pltpu.VMEM((rows, 8, width), F32),
            pltpu.VMEM((count, rows * 8, width), F32),
            pltpu.VMEM((rows, LAYERS, 8, 6 * width), F32),
            pltpu.VMEM((rows, LAYERS, 8, 6 * width), F32),
            pltpu.VMEM((count, LAYERS, 8, 6 * width), F32),
            dma(2, rows), dma(count), dma(count), dma(count),
            dma(2, rows), dma(count), dma(count), dma(count),
            dma(2, rows),
        ],
        1, 1,
    )
    mods = mod_all[:, :, 0].reshape(count, LAYERS, 6, width).transpose(1, 0, 3, 2)
    mod_full = mods.reshape(LAYERS, D, 6)
    mod_own = lax.dynamic_index_in_dim(mods, lax.axis_index("col"), 1, keepdims=False)

    stream = tokens.astype(F32).T
    saved = []
    for i in range(LAYERS):
        bias = jnp.concatenate([b_qv[i, 0], jnp.zeros_like(b_qv[i, 0]), b_qv[i, 1]])[:, None]
        normed1, inverse1, hidden1, qkv, log_total, attended, branch1, stream, w_out, w_one = run(
            functools.partial(attention_forward, sizes), 1,
            (
                stream, mod_full[i], mod_own[i], w_qkv, bias,
                attention_output_bias[i][:, None], shards[i][1], shards[i][2],
            ),
            [
                ((D, length), F32),
                ((1, length), F32),
                ((D, length), BF16),
                ((3 * heads, HEAD, length), BF16),
                ((heads, 1, length), F32),
                ((rows, rows_in, length), BF16),
                ((width, length), F32),
                ((width, length), F32),
                (shape_out, BF16),
                (shape_one, BF16),
            ],
            gather_scratch(count, (width, width), length)
            + [pltpu.VMEM(shape_out, BF16), dma(2, rows), dma(2, rows)],
            2, 1,
        )
        more = i + 1 < LAYERS
        results = run(
            functools.partial(mlp_forward, sizes, more), 2 if more else 3,
            (
                stream, mod_full[i], mod_own[i], w_one, first_linear_bias[i][:, None],
                second_linear_bias[i][:, None], shards[i][3],
            )
            + (shards[i + 1][:1] if more else ()),
            [
                ((D, length), F32),
                ((1, length), F32),
                ((D, length), BF16),
                ((hidden_width, length), F32),
                ((rows, rows_fed, length), BF16),
                ((width, length), F32),
                ((width, length), F32),
                (shape_two, BF16),
            ]
            + ([(shape_qkv, BF16)] if more else []),
            gather_scratch(count, (width, hidden_width), length)
            + [pltpu.VMEM(shape_two, BF16), dma(2, rows)]
            + ([dma(2, rows)] if more else []),
            2 if more else 1, 1 if more else 0,
        )
        normed2, inverse2, hidden2, pre, activated, branch2, stream, w_two = results[:8]
        saved.append(
            (
                normed1, inverse1, hidden1, qkv, log_total, attended, branch1,
                normed2, inverse2, hidden2, pre, activated, branch2,
                w_qkv, w_out, w_one, w_two,
            )
        )
        if more:
            w_qkv = results[8]
    output = stream.T.astype(BF16)

    grad = cotangent.astype(F32).T
    grad_mods = [None] * LAYERS
    biases = [None] * LAYERS
    grads_qkv = [None] * LAYERS
    grads_out = [None] * LAYERS
    grads_one = [None] * LAYERS
    grads_two = [None] * LAYERS
    waiting = None
    for i in reversed(range(LAYERS)):
        (
            normed1, inverse1, hidden1, qkv, log_total, attended, branch1,
            normed2, inverse2, hidden2, pre, activated, branch2,
            w_qkv, w_out, w_one, w_two,
        ) = saved[i]
        more = waiting is not None
        results = run(
            functools.partial(mlp_backward, sizes, more), 6 if more else 4,
            (grad, mod_full[i], mod_own[i], branch2, pre, normed2, inverse2, w_one, w_two, activated)
            + (waiting if more else ()),
            [
                ((width, length), BF16),
                ((hidden_width, length), BF16),
                ((width, length), F32),
                ((width, 4), F32),
                ((hidden_width, 1), F32),
                (shape_two[1:], F32),
            ]
            + ([(shape_qkv[1:], F32)] if more else []),
            scatter_scratch(count, (hidden_width, width), length)
            + sum_scratch(shape_two, *([shape_qkv] if more else [])),
        )
        grad_branch2, grad_pre, grad, sums2, sums_pre, grads_two[i] = results[:6]
        if more:
            grads_qkv[i + 1] = results[6]
        grad_branch1, grad_qkv, grad, sums1, sums_qkv, grads_out[i], grads_one[i] = run(
            functools.partial(attention_backward, sizes), 5,
            (
                grad, mod_full[i], mod_own[i], branch1, qkv, log_total, normed1, inverse1,
                w_qkv, w_out, attended, hidden2, grad_pre,
            ),
            [
                ((width, length), BF16),
                ((3 * width, length), BF16),
                ((width, length), F32),
                ((width, 4), F32),
                ((3 * width, 1), F32),
                (shape_out[1:], F32),
                (shape_one[1:], F32),
            ],
            scatter_scratch(count, (width, width), length) + sum_scratch(shape_out, shape_one),
        )
        waiting = (hidden1, grad_qkv)
        grad_mods[i] = jnp.concatenate([sums1[:, 0:3], sums2[:, 0:3]], axis=1).T.astype(BF16)
        biases[i] = jnp.concatenate(
            [sums_qkv[:width, 0], sums_qkv[2 * width :, 0], sums1[:, 3], sums2[:, 3], sums_pre[:, 0]]
        )
    mod_grad = jnp.stack(grad_mods).reshape(LAYERS, 1, 6 * width).astype(F32)
    bias_grad = jnp.stack(biases).reshape(1, -1)
    mod_grad_all, bias_sum, grad_signal, grads_qkv[0] = run(
        functools.partial(modulation_end, sizes), 7,
        (
            jnp.broadcast_to(mod_grad, (LAYERS, 8, 6 * width)),
            jnp.broadcast_to(bias_grad, (8, bias_grad.shape[1])),
            w_mod_flat,
        )
        + waiting,
        [
            ((rows, LAYERS, 8, 6 * width), F32),
            ((8, bias_grad.shape[1]), F32),
            ((8, rows_in), F32),
            (shape_qkv[1:], F32),
        ],
        [
            pltpu.VMEM((rows, LAYERS, 8, 6 * width), F32),
            pltpu.VMEM((rows, 8, bias_grad.shape[1]), F32),
            pltpu.VMEM((count, rows * 8, rows_in), F32),
            pltpu.VMEM((rows * 8, rows_in), F32),
            pltpu.VMEM((rows, rows * 8, rows_in), F32),
            dma(2, rows), dma(2, rows), dma(count), dma(count), dma(count), dma(2, rows),
        ]
        + sum_scratch(shape_qkv),
    )
    signals = signal_part.reshape(per_row, rows, 8, width)[:, :, 0]
    signals = signals.transpose(1, 0, 2).reshape(rows, rows_in)
    mod_rows = mod_grad_all[:, :, 0]
    mod_rows = mod_rows.reshape(rows, LAYERS, 6, width)
    grad_w_mod = sum(
        signals[r][None, :, None, None] * mod_rows[r][:, None] for r in range(rows)
    )
    grad_b_mod = jnp.sum(mod_rows, 0)
    grad_signal = lax.dynamic_slice(
        grad_signal[:1], (0, lax.axis_index("col") % per_row * width), (1, width)
    )
    grad_cond = jax.vjp(jax.nn.silu, cond_float)[1](grad_signal)[0]
    bias_sum = bias_sum[0].reshape(LAYERS, -1)
    return (
        output,
        grad.T,
        grad_cond,
        grad_w_mod,
        grad_b_mod,
        jnp.stack(grads_qkv).reshape(LAYERS, rows_in, 3, width),
        bias_sum[:, : 2 * width].reshape(LAYERS, 2, width),
        jnp.stack([one.T for one in grads_out]),
        bias_sum[:, 2 * width : 3 * width],
        jnp.stack(grads_one),
        bias_sum[:, 4 * width :],
        jnp.stack([one.T for one in grads_two]),
        bias_sum[:, 3 * width : 4 * width],
    )


def solution(mesh):
    in_specs = (
        P("row", "col"),
        P("row", "col"),
        P(None, "row", None, "col"),
        P(None, None, "col"),
        P(None, "row", None, "col"),
        P(None, None, "col"),
        P(None, "row", "col"),
        P(None, "col"),
        P(None, "row", "col"),
        P(None, "col"),
        P(None, "row", "col"),
        P(None, "col"),
        P("row", "col"),
    )
    out_specs = (
        P("row", "col"),
        P("row", "col"),
        P("row", "col"),
        P(None, "row", None, "col"),
        P(None, None, "col"),
        P(None, "row", None, "col"),
        P(None, None, "col"),
        P(None, "row", "col"),
        P(None, "col"),
        P(None, "row", "col"),
        P(None, "col"),
        P(None, "row", "col"),
        P(None, "col"),
    )
    return jax.shard_map(
        functools.partial(per_device, (mesh.shape["row"], mesh.shape["col"])),
        mesh=mesh,
        in_specs=in_specs,
        out_specs=out_specs,
        check_vma=False,
    )
```

```python
import functools
import math

import jax
import jax.numpy as jnp
from jax import lax
from jax.experimental import pallas as pl
from jax.experimental.pallas import tpu as pltpu
from jax.sharding import PartitionSpec as P

D = 1152
HEAD = 72
LAYERS = 2
EPS = 1e-06
SCALE = HEAD ** (-0.5)
BF16 = jnp.bfloat16
F32 = jnp.float32
MESH = pl.DeviceIdType.MESH
VMEM_BYTES = 52 * 1024 * 1024


def nn(a, b):
    return lax.dot_general(a, b, (((1,), (0,)), ((), ())), preferred_element_type=F32)


def tn(a, b):
    return lax.dot_general(a, b, (((0,), (0,)), ((), ())), preferred_element_type=F32)


def nt(a, b):
    return lax.dot_general(a, b, (((1,), (1,)), ((), ())), preferred_element_type=F32)


def flat(x):
    blocks, rows, columns = x.shape
    if rows % 16 == 0:
        return x.reshape(blocks * rows, columns)
    return x.astype(F32).reshape(blocks * rows, columns).astype(x.dtype)


class Place:
    def __init__(self, sizes):
        rows, count = sizes
        self.rows = rows
        self.per_row = count // rows
        self.row = lax.axis_index("row")
        self.col = lax.axis_index("col")
        self.count = count
        self.zs = count // 2
        self.z = self.col // 2
        self.core = self.col % 2
        self.mate_core = 1 - self.core
        self.mate = (self.row, self.z * 2 + self.mate_core)

    def ahead(self, k):
        return lax.rem(self.z + k, self.zs)

    def behind(self, k):
        return lax.rem(self.z + self.zs - k, self.zs)

    def peer(self, z):
        return (self.row, z * 2 + self.core)

    def below(self, k):
        return lax.rem(self.row + k, self.rows)

    def above(self, k):
        return lax.rem(self.row + self.rows - k, self.rows)


def greet(here, with_rows=True):
    barrier = pltpu.get_barrier_semaphore()
    pl.semaphore_signal(barrier, inc=1, device_id=here.mate, device_id_type=MESH)
    for k in range(1, here.zs):
        pl.semaphore_signal(
            barrier, inc=1, device_id=here.peer(here.ahead(k)), device_id_type=MESH
        )
    if with_rows:
        for k in range(1, here.rows):
            pl.semaphore_signal(
                barrier, inc=1, device_id=(here.below(k), here.col), device_id_type=MESH
            )
        pl.semaphore_wait(barrier, here.zs + here.rows - 1)
    else:
        pl.semaphore_wait(barrier, here.zs)


def send(src, dst, send_sem, recv_sem, device):
    return pltpu.make_async_remote_copy(
        src_ref=src,
        dst_ref=dst,
        send_sem=send_sem,
        recv_sem=recv_sem,
        device_id=device,
        device_id_type=MESH,
    )


def gather(here, buf, out_sem, fwd_sem, in_sem):
    own = here.col
    started = []
    for k in range(1, here.zs):
        copy = send(
            buf.at[own], buf.at[own], out_sem.at[k], in_sem.at[own], here.peer(here.ahead(k))
        )
        copy.start()
        started.append(copy)
    copy = send(buf.at[own], buf.at[own], out_sem.at[0], in_sem.at[own], here.mate)
    copy.start()
    started.append(copy)
    for k in range(1, here.zs):
        src = here.behind(k) * 2 + here.core
        copy = send(buf.at[src], buf.at[src], fwd_sem.at[k], in_sem.at[src], here.mate)
        copy.wait_recv()
        copy.start()
        started.append(copy)
    for k in range(here.zs):
        src = here.behind(k) * 2 + here.mate_core
        send(buf.at[src], buf.at[src], fwd_sem.at[0], in_sem.at[src], here.mate).wait_recv()
    for copy in started:
        copy.wait_send()


class RowGather:
    def __init__(self, here, src, dst, sems):
        self.here, self.src, self.dst = here, src, dst
        self.out, self.into = sems.at[0], sems.at[1]
        own = here.row
        self.local = pltpu.make_async_copy(src, dst.at[own], self.out.at[0])
        self.local.start()
        self.copies = []
        for k in range(1, here.rows):
            copy = send(
                src, dst.at[own], self.out.at[k], self.into.at[own], (here.below(k), here.col)
            )
            copy.start()
            self.copies.append(copy)

    def finish(self):
        here = self.here
        self.local.wait()
        for k in range(1, here.rows):
            src = here.above(k)
            send(
                self.src, self.dst.at[src], self.out.at[k], self.into.at[src], (src, here.col)
            ).wait_recv()
        for copy in self.copies:
            copy.wait_send()


class RowSum:
    def __init__(self, here, parts, got, sems):
        self.here, self.parts, self.got = here, parts, got
        self.out, self.into = sems.at[0], sems.at[1]
        self.copies = []
        for k in range(1, here.rows):
            to = here.below(k)
            copy = send(
                parts.at[to],
                got.at[here.row],
                self.out.at[k],
                self.into.at[here.row],
                (to, here.col),
            )
            copy.start()
            self.copies.append(copy)

    def finish(self):
        here = self.here
        total = self.parts[here.row].astype(F32)
        for k in range(1, here.rows):
            src = here.above(k)
            send(
                self.parts.at[src],
                self.got.at[src],
                self.out.at[k],
                self.into.at[src],
                (src, here.col),
            ).wait_recv()
            total = total + self.got[src].astype(F32)
        for copy in self.copies:
            copy.wait_send()
        return total


def in_grad(here, hidden, grad, scratch):
    parts, got, sems = scratch
    depth = parts.shape[1]
    product = nt(hidden[...], grad[...])
    for r in range(here.rows):
        parts[r] = product[r * depth : (r + 1) * depth].astype(BF16)
    return RowSum(here, parts, got, sems)


def fed_grad(here, fed, grad, scratch):
    parts, got, sems = scratch
    grad_now = grad[...]
    for r in range(here.rows):
        parts[r] = nt(grad_now, fed[r]).astype(BF16)
    return RowSum(here, parts, got, sems)


def gather_chain(here, buf, out_sem, fwd_sem, in_sem):
    z, zs, core = here.z, here.zs, here.core
    above, below = here.peer(here.ahead(1)), here.peer(here.behind(1))

    def go(src, device, sem):
        return send(buf.at[src], buf.at[src], sem, in_sem.at[src], device)

    own = here.col
    pl.when(z < zs - 1)(lambda: go(own, above, out_sem.at[0]).start())
    pl.when(z > 0)(lambda: go(own, below, out_sem.at[zs]).start())
    go(own, here.mate, fwd_sem.at[z]).start()

    def pass_on(src_z, further, device, sem):
        src = src_z * 2 + core
        go(src, device, sem).wait_recv()
        pl.when(further)(lambda: go(src, device, sem).start())
        go(src, here.mate, fwd_sem.at[src_z]).start()

    for k in range(1, zs):
        pl.when(z >= k)(
            functools.partial(pass_on, here.behind(k), z < zs - 1, above, out_sem.at[k])
        )
        pl.when(z + k < zs)(
            functools.partial(pass_on, here.ahead(k), z > 0, below, out_sem.at[zs + k])
        )
    for k in range(zs):
        src = here.behind(k) * 2 + here.mate_core
        go(src, here.mate, fwd_sem.at[here.behind(k)]).wait_recv()
    for k in range(zs):
        go(own, here.mate, fwd_sem.at[k]).wait_send()
        pl.when((z >= k) & (z < zs - 1))(lambda: go(own, above, out_sem.at[k]).wait_send())
        pl.when((z + k < zs) & (z > 0))(lambda: go(own, below, out_sem.at[zs + k]).wait_send())


def scatter_chain(here, parts, near, up, down, near_sems, up_sems, down_sems, meanwhile):
    near_out, near_in = near_sems
    z, zs, core = here.z, here.zs, here.core
    above, below = here.peer(here.ahead(1)), here.peer(here.behind(1))

    def swap(d):
        return send(
            parts.at[here.mate_core, d], near.at[d], near_out.at[d], near_in.at[d], here.mate
        )

    def hop(d, buf, sems, device):
        return send(parts.at[core, d], buf.at[d], sems[0].at[d], sems[1].at[d], device)

    order = []
    for i in range(zs - 1):
        order += [(zs - 1 - i, True), (i, False)]
    sent = []
    for d, _ in order:
        if d not in sent:
            sent.append(d)
            swap(d).start()

    @pl.when(z == 0)
    def _():
        up[0] = jnp.zeros(up.shape[1:], BF16)

    @pl.when(z == zs - 1)
    def _():
        down[zs - 1] = jnp.zeros(down.shape[1:], BF16)

    def one(d, buf, sems, device, first):
        swap(d).wait_recv()
        both = parts[core, d].astype(F32) + near[d].astype(F32)

        @pl.when(first)
        def _():
            parts[core, d] = both.astype(BF16)

        @pl.when(jnp.logical_not(first))
        def _():
            hop(d, buf, sems, device).wait_recv()
            parts[core, d] = (both + buf[d].astype(F32)).astype(BF16)

        hop(d, buf, sems, device).start()

    for i, (d, upward) in enumerate(order):
        if upward:
            pl.when(z < d)(functools.partial(one, d, up, up_sems, above, z == 0))
        else:
            pl.when(z > d)(functools.partial(one, d, down, down_sems, below, z == zs - 1))
        if i == 1:
            meanwhile()
    swap(z).wait_recv()
    total = parts[core, z].astype(F32) + near[z].astype(F32)
    pl.when(z > 0)(lambda: hop(z, up, up_sems, above).wait_recv())
    pl.when(z < zs - 1)(lambda: hop(z, down, down_sems, below).wait_recv())
    total = total + up[z].astype(F32) + down[z].astype(F32)
    for d in range(zs):
        swap(d).wait_send()
        pl.when(z < d)(lambda: hop(d, up, up_sems, above).wait_send())
        pl.when(z > d)(lambda: hop(d, down, down_sems, below).wait_send())
    return total


def scatter_sum(here, parts, near, far, near_sems, far_sems, stat=None, meanwhile=None):
    near_out, near_in = near_sems
    far_out, far_in = far_sems
    z, core = here.z, here.core
    order = list(range(1, here.zs)) + [0]
    near_copies = []
    if stat is not None:
        own, got, sums, others, stat_sems = stat
        stat_out, stat_in = stat_sems
        first = send(own, got, stat_out.at[0], stat_in.at[z], here.mate)
        first.start()
    for k in order:
        to = here.ahead(k)
        copy = send(
            parts.at[here.mate_core, to], near.at[to], near_out.at[k], near_in.at[to], here.mate
        )
        copy.start()
        near_copies.append(copy)
    far_copies = []
    if stat is not None:
        first.wait()
        sums[...] = own[...] + got[...]
        for k in range(1, here.zs):
            copy = send(
                sums, others.at[z], stat_out.at[k], stat_in.at[z], here.peer(here.ahead(k))
            )
            copy.start()
            far_copies.append(copy)
    total = None
    for i, k in enumerate(order):
        to = here.ahead(k)
        near_copies[i].wait_recv()
        both = parts[core, to].astype(F32) + near[to].astype(F32)
        if k == 0:
            total = both
        else:
            parts[core, to] = both.astype(BF16)
            copy = send(
                parts.at[core, to], far.at[z], far_out.at[k], far_in.at[z], here.peer(to)
            )
            copy.start()
            far_copies.append(copy)
    if meanwhile is not None:
        meanwhile()
    stat_total = None
    if stat is not None:
        stat_total = sums[...]
        for k in range(1, here.zs):
            src = here.behind(k)
            send(
                sums, others.at[src], stat_out.at[k], stat_in.at[src], here.peer(src)
            ).wait_recv()
            stat_total = stat_total + others[src]
    for k in range(1, here.zs):
        src = here.behind(k)
        send(
            parts.at[core, src], far.at[src], far_out.at[k], far_in.at[src], here.peer(src)
        ).wait_recv()
        total = total + far[src].astype(F32)
    for copy in near_copies:
        copy.wait_send()
    for copy in far_copies:
        copy.wait_send()
    return total, stat_total


def normalize(stream):
    average = jnp.sum(stream, 0, keepdims=True) / D
    centred = stream - average
    spread = jnp.sum(centred * centred, 0, keepdims=True) / D
    inverse = lax.rsqrt(spread + EPS)
    return centred * inverse, inverse


def gelu(u):
    inner = math.sqrt(2 / math.pi) * (u + 0.044715 * (u * u * u))
    return 0.5 * u * (1.0 + jnp.tanh(inner))


def gelu_slope(u):
    root = math.sqrt(2 / math.pi)
    t = jnp.tanh(root * (u + 0.044715 * (u * u * u)))
    return 0.5 * (1.0 + t) + 0.5 * u * (1.0 - t * t) * (root * (1.0 + 3 * 0.044715 * (u * u)))


def fed_product(here, weight, buf, kept):
    total = 0.0
    for r in range(here.rows):
        piece = flat(buf[r * here.per_row : (r + 1) * here.per_row])
        kept[r] = piece
        total = total + nn(weight[r], piece)
    return total


def attention_forward(
    sizes, stream, mod, mod_own, w_qkv, b_qkv, b_out, fed, next_in,
    normed, inverse, hidden, qkv, log_total, attended, branch, stream_out, w_out, all_in,
    x_buf, a_buf, x_out, x_fwd, x_in, a_out, a_fwd, a_in, w_buf, fed_sems, in_sems,
):
    here = Place(sizes)
    greet(here)
    needed = RowGather(here, fed, w_buf, fed_sems)
    coming = RowGather(here, next_in, all_in, in_sems)
    x_buf[here.col] = stream[...].astype(BF16)
    gather(here, x_buf, x_out, x_fwd, x_in)
    values, inv = normalize(flat(x_buf[...]).astype(F32))
    normed[...] = values
    inverse[...] = inv
    hidden_now = (values * (1.0 + mod[:, 1:2]) + mod[:, 0:1]).astype(BF16)
    hidden[...] = hidden_now
    projected = tn(flat(w_qkv[...]), hidden_now) + b_qkv[...]
    heads = qkv.shape[0] // 3
    for i in range(3 * heads):
        qkv[i] = projected[i * HEAD : (i + 1) * HEAD].astype(BF16)
    pieces = []
    for h in range(heads):
        scores = tn(qkv[heads + h], qkv[h]) * SCALE
        highest = jnp.max(scores, axis=0, keepdims=True)
        expd = jnp.exp(scores - highest)
        summed = jnp.sum(expd, axis=0, keepdims=True)
        log_total[h] = highest + jnp.log(summed)
        probs = (expd / summed).astype(BF16)
        pieces.append(nn(qkv[2 * heads + h], probs))
    a_buf[here.col] = jnp.concatenate(pieces, axis=0).astype(BF16)
    gather(here, a_buf, a_out, a_fwd, a_in)
    needed.finish()
    w_out[...] = w_buf[...]
    branch_now = b_out[...] + fed_product(here, w_buf, a_buf, attended)
    branch[...] = branch_now
    stream_out[...] = stream[...] + mod_own[:, 2:3] * branch_now
    coming.finish()


def mlp_forward(sizes, more, *refs):
    stream, mod, mod_own, w_one, b_one, b_two, fed = refs[:7]
    refs = refs[7:]
    if more:
        next_in = refs[0]
        refs = refs[1:]
    normed, inverse, hidden, pre, activated, branch, stream_out, w_two = refs[:8]
    refs = refs[8:]
    if more:
        all_in = refs[0]
        refs = refs[1:]
    x_buf, a_buf, x_out, x_fwd, x_in, a_out, a_fwd, a_in, w_buf, fed_sems = refs[:10]
    here = Place(sizes)
    greet(here)
    needed = RowGather(here, fed, w_buf, fed_sems)
    if more:
        coming = RowGather(here, next_in, all_in, refs[10])
    x_buf[here.col] = stream[...].astype(BF16)
    gather(here, x_buf, x_out, x_fwd, x_in)
    values, inv = normalize(flat(x_buf[...]).astype(F32))
    normed[...] = values
    inverse[...] = inv
    hidden_now = (values * (1.0 + mod[:, 4:5]) + mod[:, 3:4]).astype(BF16)
    hidden[...] = hidden_now
    pre_now = tn(flat(w_one[...]), hidden_now) + b_one[...]
    pre[...] = pre_now
    a_buf[here.col] = gelu(pre_now).astype(BF16)
    gather_chain(here, a_buf, a_out, a_fwd, a_in)
    needed.finish()
    w_two[...] = w_buf[...]
    branch_now = b_two[...] + fed_product(here, w_buf, a_buf, activated)
    branch[...] = branch_now
    stream_out[...] = stream[...] + mod_own[:, 5:6] * branch_now
    if more:
        coming.finish()


def split_parts(here, parts, weight, rows):
    size = parts.shape[2]
    for r in range(here.rows):
        product = tn(weight[r], rows)
        for j in range(here.per_row):
            c = r * here.per_row + j
            parts[c % 2, c // 2] = product[j * size : (j + 1) * size].astype(BF16)


def split_norm_parts(here, parts, stat, weight, rows, normed, gain):
    size = parts.shape[2]
    product = nn(flat(weight[...]), rows)
    for c in range(here.count):
        parts[c % 2, c // 2] = product[c * size : (c + 1) * size].astype(BF16)
    scaled = product * (1.0 + gain)
    stat[...] = jnp.zeros_like(stat)
    stat[0:1] = jnp.sum(scaled, 0, keepdims=True)
    stat[1:2] = jnp.sum(scaled * normed[...], 0, keepdims=True)


def norm_back(here, grad_hidden, totals, normed, inverse, gain):
    width = grad_hidden.shape[0]
    own = normed[pl.ds(pl.multiple_of(here.col * width, 8), width)]
    scaled = grad_hidden * (1.0 + gain)
    change = inverse[...] * (scaled - totals[0:1] / D - own * (totals[1:2] / D))
    shift = jnp.sum(grad_hidden, 1, keepdims=True)
    stretch = jnp.sum(grad_hidden * own, 1, keepdims=True)
    return change, shift, stretch


def mlp_backward(sizes, more, *refs):
    grad, mod, mod_own, branch, pre, normed, inverse, w_one, w_two, activated = refs[:10]
    refs = refs[10:]
    if more:
        feeds = refs[:2]
        refs = refs[2:]
    grad_branch, grad_pre, grad_out, sums, sums_pre, weight_fed = refs[:6]
    refs = refs[6:]
    if more:
        weight_in = refs[0]
        refs = refs[1:]
    a_parts, a_near, a_far, h_parts, h_near, h_far, stat_own, stat_got, stat_sum, stat_far = refs[:10]
    an_out, an_in, af_out, af_in, hn_out, hn_in, hf_out, hf_in, st_out, st_in = refs[10:20]
    a_down, ad_out, ad_in = refs[20:23]
    here = Place(sizes)
    greet(here)
    going = []

    def meanwhile():
        going.append(fed_grad(here, activated, grad_branch, refs[23:26]))
        if more:
            going.append(in_grad(here, *feeds, refs[26:29]))

    grad_now = grad[...]
    grad_branch_now = (mod_own[:, 5:6] * grad_now).astype(BF16)
    grad_branch[...] = grad_branch_now
    split_parts(here, a_parts, w_two, grad_branch_now)
    grad_act = scatter_chain(
        here, a_parts, a_near, a_far, a_down,
        (an_out, an_in), (af_out, af_in), (ad_out, ad_in), meanwhile,
    )
    grad_pre_now = (grad_act * gelu_slope(pre[...])).astype(BF16)
    grad_pre[...] = grad_pre_now
    split_norm_parts(here, h_parts, stat_own, w_one, grad_pre_now, normed, mod[:, 4:5])
    grad_hidden, totals = scatter_sum(
        here, h_parts, h_near, h_far, (hn_out, hn_in), (hf_out, hf_in),
        (stat_own, stat_got, stat_sum, stat_far, (st_out, st_in)),
    )
    change, shift, stretch = norm_back(
        here, grad_hidden, totals, normed, inverse, mod_own[:, 4:5]
    )
    grad_out[...] = grad_now + change
    sums[:, 0:1] = shift
    sums[:, 1:2] = stretch
    sums[:, 2:3] = jnp.sum(grad_now * branch[...], 1, keepdims=True)
    sums[:, 3:4] = jnp.sum(grad_branch_now.astype(F32), 1, keepdims=True)
    sums_pre[...] = jnp.sum(grad_pre_now.astype(F32), 1, keepdims=True)
    weight_fed[...] = going[0].finish()
    if more:
        weight_in[...] = going[1].finish()


def attention_backward(
    sizes, grad, mod, mod_own, branch, qkv, log_total, normed, inverse, w_qkv, w_out,
    attended, hidden_two, grad_pre,
    grad_branch, grad_qkv, grad_out, sums, sums_qkv, weight_fed, weight_in,
    a_parts, a_near, a_far, h_parts, h_near, h_far, stat_own, stat_got, stat_sum, stat_far,
    an_out, an_in, af_out, af_in, hn_out, hn_in, hf_out, hf_in, st_out, st_in, *row_scratch,
):
    here = Place(sizes)
    greet(here)
    going = []

    def meanwhile():
        going.append(fed_grad(here, attended, grad_branch, row_scratch[:3]))
        going.append(in_grad(here, hidden_two, grad_pre, row_scratch[3:]))

    grad_now = grad[...]
    grad_branch_now = (mod_own[:, 2:3] * grad_now).astype(BF16)
    grad_branch[...] = grad_branch_now
    split_parts(here, a_parts, w_out, grad_branch_now)
    grad_att, _ = scatter_sum(
        here, a_parts, a_near, a_far, (an_out, an_in), (af_out, af_in), None, meanwhile
    )
    heads = qkv.shape[0] // 3
    queries, keys, values = [], [], []
    for h in range(heads):
        query, key, value = qkv[h], qkv[heads + h], qkv[2 * heads + h]
        grad_one = grad_att[h * HEAD : (h + 1) * HEAD].astype(BF16)
        weights = jnp.exp(tn(key, query) * SCALE - log_total[h])
        grad_weights = tn(value, grad_one)
        values.append(nt(grad_one, weights.astype(BF16)))
        inner = jnp.sum(weights * grad_weights, axis=0, keepdims=True)
        grad_scores = (weights * (grad_weights - inner)).astype(BF16)
        queries.append(nn(key, grad_scores) * SCALE)
        keys.append(nt(query, grad_scores) * SCALE)
    grad_qkv_now = jnp.concatenate(queries + keys + values, axis=0).astype(BF16)
    grad_qkv[...] = grad_qkv_now
    split_norm_parts(here, h_parts, stat_own, w_qkv, grad_qkv_now, normed, mod[:, 1:2])
    grad_hidden, totals = scatter_sum(
        here, h_parts, h_near, h_far, (hn_out, hn_in), (hf_out, hf_in),
        (stat_own, stat_got, stat_sum, stat_far, (st_out, st_in)),
    )
    change, shift, stretch = norm_back(
        here, grad_hidden, totals, normed, inverse, mod_own[:, 1:2]
    )
    grad_out[...] = grad_now + change
    sums[:, 0:1] = shift
    sums[:, 1:2] = stretch
    sums[:, 2:3] = jnp.sum(grad_now * branch[...], 1, keepdims=True)
    sums[:, 3:4] = jnp.sum(grad_branch_now.astype(F32), 1, keepdims=True)
    sums_qkv[...] = jnp.sum(grad_qkv_now.astype(F32), 1, keepdims=True)
    weight_fed[...] = going[0].finish()
    weight_in[...] = going[1].finish()


def modulation_start(
    sizes, signal, w_mod, b_mod, next_in,
    mod_all, signal_part, all_in,
    sig_row, sig_col, mod_part, mod_got, mod_col,
    sig_row_sems, s_out, s_fwd, s_in, mod_sems, m_out, m_fwd, m_in, in_sems,
):
    here = Place(sizes)
    greet(here)
    width = signal.shape[1]
    signals = RowGather(here, signal, sig_row, sig_row_sems)
    coming = RowGather(here, next_in, all_in, in_sems)
    signals.finish()
    sig_col[here.col] = sig_row[...].reshape(here.rows * 8, width)
    gather(here, sig_col, s_out, s_fwd, s_in)
    for j in range(here.per_row):
        signal_part[j] = sig_col[here.row * here.per_row + j]
    for i in range(LAYERS):
        product = 0.0
        for j in range(here.per_row):
            product = product + nn(
                signal_part[j].astype(BF16), w_mod[i, j * width : (j + 1) * width]
            )
        for r in range(here.rows):
            mod_part[r, i] = product[r * 8 : (r + 1) * 8]
    total = RowSum(here, mod_part, mod_got, mod_sems).finish() + b_mod[...]
    mod_col[here.col] = total
    gather(here, mod_col, m_out, m_fwd, m_in)
    mod_all[...] = mod_col[...]
    coming.finish()


def modulation_end(
    sizes, grad_mod, biases, w_mod, hidden, grad_qkv,
    mod_all, bias_sum, grad_signal, weight_in,
    mod_row, bias_row, back_col, back_own, back_row,
    mod_sems, bias_sems, b_out, b_fwd, b_in, back_sems, *row_scratch,
):
    here = Place(sizes)
    greet(here)
    mods = RowGather(here, grad_mod, mod_row, mod_sems)
    shares = RowGather(here, biases, bias_row, bias_sems)
    going = in_grad(here, hidden, grad_qkv, row_scratch)
    mods.finish()
    mod_all[...] = mod_row[...]
    product = 0.0
    for i in range(LAYERS):
        rows = mod_row[:, i].reshape(here.rows * 8, mod_row.shape[3])
        product = product + nt(rows.astype(BF16), w_mod[i])
    back_col[here.col] = product
    gather(here, back_col, b_out, b_fwd, b_in)
    back_own[...] = jnp.sum(back_col[...], axis=0)
    backs = RowGather(here, back_own, back_row, back_sems)
    shares.finish()
    bias_sum[...] = jnp.sum(bias_row[...], axis=0)
    backs.finish()
    grad_signal[...] = back_row[
        here.col // here.per_row, pl.ds(pl.multiple_of(here.row * 8, 8), 8)
    ]
    weight_in[...] = going.finish()


def run(body, ident, args, outs, scratch, far_args=0, far_outs=0):
    vmem = pl.BlockSpec(memory_space=pltpu.VMEM)
    anywhere = pl.BlockSpec(memory_space=pl.ANY)
    return pl.pallas_call(
        body,
        out_shape=[jax.ShapeDtypeStruct(shape, dtype) for shape, dtype in outs],
        in_specs=[vmem] * (len(args) - far_args) + [anywhere] * far_args,
        out_specs=[vmem] * (len(outs) - far_outs) + [anywhere] * far_outs,
        scratch_shapes=scratch,
        compiler_params=pltpu.CompilerParams(
            collective_id=ident, has_side_effects=True, vmem_limit_bytes=VMEM_BYTES
        ),
    )(*args)


def dma(*shape):
    return pltpu.SemaphoreType.DMA(shape)


def gather_scratch(count, sizes, width):
    bufs = [pltpu.VMEM((count, size, width), BF16) for size in sizes]
    return bufs + [dma(count) for _ in range(3 * len(sizes))]


def scatter_scratch(count, sizes, width):
    zs = count // 2
    bufs = []
    for size in sizes:
        bufs.append(pltpu.VMEM((2, zs, size, width), BF16))
        bufs.append(pltpu.VMEM((zs, size, width), BF16))
        bufs.append(pltpu.VMEM((zs, size, width), BF16))
    bufs += [pltpu.VMEM((8, width), F32) for _ in range(3)]
    bufs.append(pltpu.VMEM((zs, 8, width), F32))
    return bufs + [dma(zs) for _ in range(4 * len(sizes) + 2)]


def per_device(
    sizes,
    tokens, cond, w_mod, b_mod, query_key_value_weight, b_qv,
    attention_output_weight, attention_output_bias, first_linear_weight, first_linear_bias,
    second_linear_weight, second_linear_bias, cotangent,
):
    rows, count = sizes
    assert cond.shape[0] == 1
    length, width = tokens.shape
    heads = width // HEAD
    hidden_width = first_linear_weight.shape[2]
    rows_in = w_mod.shape[1]
    rows_fed = second_linear_weight.shape[1]
    per_row = count // rows
    cond_float = cond.astype(F32)
    signal = jax.nn.silu(cond_float).astype(BF16).astype(F32)
    w_mod_flat = w_mod.reshape(LAYERS, rows_in, 6 * width)

    shards = []
    for i in range(LAYERS):
        shards.append(
            (
                query_key_value_weight[i].reshape(rows_in, 3 * width),
                attention_output_weight[i].T,
                first_linear_weight[i],
                second_linear_weight[i].T,
            )
        )

    shape_qkv = (rows, rows_in, 3 * width)
    shape_out = (rows, width, rows_in)
    shape_one = (rows, rows_in, hidden_width)
    shape_two = (rows, width, rows_fed)

    def sum_scratch(*shapes):
        scratch = []
        for shape in shapes:
            scratch += [pltpu.VMEM(shape, BF16), pltpu.VMEM(shape, BF16), dma(2, rows)]
        return scratch

    mod_all, signal_part, w_qkv = run(
        functools.partial(modulation_start, sizes), 0,
        (
            jnp.broadcast_to(signal, (8, width)),
            w_mod_flat,
            b_mod.reshape(LAYERS, 1, 6 * width),
            shards[0][0],
        ),
        [
            ((count, LAYERS, 8, 6 * width), F32),
            ((per_row, rows * 8, width), F32),
            (shape_qkv, BF16),
        ],
        [
            pltpu.VMEM((rows, 8, width), F32),
            pltpu.VMEM((count, rows * 8, width), F32),
            pltpu.VMEM((rows, LAYERS, 8, 6 * width), F32),
            pltpu.VMEM((rows, LAYERS, 8, 6 * width), F32),
            pltpu.VMEM((count, LAYERS, 8, 6 * width), F32),
            dma(2, rows), dma(count), dma(count), dma(count),
            dma(2, rows), dma(count), dma(count), dma(count),
            dma(2, rows),
        ],
        1, 1,
    )
    mods = mod_all[:, :, 0].reshape(count, LAYERS, 6, width).transpose(1, 0, 3, 2)
    mod_full = mods.reshape(LAYERS, D, 6)
    mod_own = lax.dynamic_index_in_dim(mods, lax.axis_index("col"), 1, keepdims=False)

    stream = tokens.astype(F32).T
    saved = []
    for i in range(LAYERS):
        bias = jnp.concatenate([b_qv[i, 0], jnp.zeros_like(b_qv[i, 0]), b_qv[i, 1]])[:, None]
        normed1, inverse1, hidden1, qkv, log_total, attended, branch1, stream, w_out, w_one = run(
            functools.partial(attention_forward, sizes), 1,
            (
                stream, mod_full[i], mod_own[i], w_qkv, bias,
                attention_output_bias[i][:, None], shards[i][1], shards[i][2],
            ),
            [
                ((D, length), F32),
                ((1, length), F32),
                ((D, length), BF16),
                ((3 * heads, HEAD, length), BF16),
                ((heads, 1, length), F32),
                ((rows, rows_in, length), BF16),
                ((width, length), F32),
                ((width, length), F32),
                (shape_out, BF16),
                (shape_one, BF16),
            ],
            gather_scratch(count, (width, width), length)
            + [pltpu.VMEM(shape_out, BF16), dma(2, rows), dma(2, rows)],
            2, 1,
        )
        more = i + 1 < LAYERS
        results = run(
            functools.partial(mlp_forward, sizes, more), 2 if more else 3,
            (
                stream, mod_full[i], mod_own[i], w_one, first_linear_bias[i][:, None],
                second_linear_bias[i][:, None], shards[i][3],
            )
            + (shards[i + 1][:1] if more else ()),
            [
                ((D, length), F32),
                ((1, length), F32),
                ((D, length), BF16),
                ((hidden_width, length), F32),
                ((rows, rows_fed, length), BF16),
                ((width, length), F32),
                ((width, length), F32),
                (shape_two, BF16),
            ]
            + ([(shape_qkv, BF16)] if more else []),
            gather_scratch(count, (width, hidden_width), length)
            + [pltpu.VMEM(shape_two, BF16), dma(2, rows)]
            + ([dma(2, rows)] if more else []),
            2 if more else 1, 1 if more else 0,
        )
        normed2, inverse2, hidden2, pre, activated, branch2, stream, w_two = results[:8]
        saved.append(
            (
                normed1, inverse1, hidden1, qkv, log_total, attended, branch1,
                normed2, inverse2, hidden2, pre, activated, branch2,
                w_qkv, w_out, w_one, w_two,
            )
        )
        if more:
            w_qkv = results[8]
    output = stream.T.astype(BF16)

    grad = cotangent.astype(F32).T
    grad_mods = [None] * LAYERS
    biases = [None] * LAYERS
    grads_qkv = [None] * LAYERS
    grads_out = [None] * LAYERS
    grads_one = [None] * LAYERS
    grads_two = [None] * LAYERS
    waiting = None
    for i in reversed(range(LAYERS)):
        (
            normed1, inverse1, hidden1, qkv, log_total, attended, branch1,
            normed2, inverse2, hidden2, pre, activated, branch2,
            w_qkv, w_out, w_one, w_two,
        ) = saved[i]
        more = waiting is not None
        results = run(
            functools.partial(mlp_backward, sizes, more), 6 if more else 4,
            (grad, mod_full[i], mod_own[i], branch2, pre, normed2, inverse2, w_one, w_two, activated)
            + (waiting if more else ()),
            [
                ((width, length), BF16),
                ((hidden_width, length), BF16),
                ((width, length), F32),
                ((width, 4), F32),
                ((hidden_width, 1), F32),
                (shape_two[1:], F32),
            ]
            + ([(shape_qkv[1:], F32)] if more else []),
            scatter_scratch(count, (hidden_width, width), length)
            + [pltpu.VMEM((count // 2, hidden_width, length), BF16)]
            + [dma(count // 2), dma(count // 2)]
            + sum_scratch(shape_two, *([shape_qkv] if more else [])),
        )
        grad_branch2, grad_pre, grad, sums2, sums_pre, grads_two[i] = results[:6]
        if more:
            grads_qkv[i + 1] = results[6]
        grad_branch1, grad_qkv, grad, sums1, sums_qkv, grads_out[i], grads_one[i] = run(
            functools.partial(attention_backward, sizes), 5,
            (
                grad, mod_full[i], mod_own[i], branch1, qkv, log_total, normed1, inverse1,
                w_qkv, w_out, attended, hidden2, grad_pre,
            ),
            [
                ((width, length), BF16),
                ((3 * width, length), BF16),
                ((width, length), F32),
                ((width, 4), F32),
                ((3 * width, 1), F32),
                (shape_out[1:], F32),
                (shape_one[1:], F32),
            ],
            scatter_scratch(count, (width, width), length) + sum_scratch(shape_out, shape_one),
        )
        waiting = (hidden1, grad_qkv)
        grad_mods[i] = jnp.concatenate([sums1[:, 0:3], sums2[:, 0:3]], axis=1).T.astype(BF16)
        biases[i] = jnp.concatenate(
            [sums_qkv[:width, 0], sums_qkv[2 * width :, 0], sums1[:, 3], sums2[:, 3], sums_pre[:, 0]]
        )
    mod_grad = jnp.stack(grad_mods).reshape(LAYERS, 1, 6 * width).astype(F32)
    bias_grad = jnp.stack(biases).reshape(1, -1)
    mod_grad_all, bias_sum, grad_signal, grads_qkv[0] = run(
        functools.partial(modulation_end, sizes), 7,
        (
            jnp.broadcast_to(mod_grad, (LAYERS, 8, 6 * width)),
            jnp.broadcast_to(bias_grad, (8, bias_grad.shape[1])),
            w_mod_flat,
        )
        + waiting,
        [
            ((rows, LAYERS, 8, 6 * width), F32),
            ((8, bias_grad.shape[1]), F32),
            ((8, rows_in), F32),
            (shape_qkv[1:], F32),
        ],
        [
            pltpu.VMEM((rows, LAYERS, 8, 6 * width), F32),
            pltpu.VMEM((rows, 8, bias_grad.shape[1]), F32),
            pltpu.VMEM((count, rows * 8, rows_in), F32),
            pltpu.VMEM((rows * 8, rows_in), F32),
            pltpu.VMEM((rows, rows * 8, rows_in), F32),
            dma(2, rows), dma(2, rows), dma(count), dma(count), dma(count), dma(2, rows),
        ]
        + sum_scratch(shape_qkv),
    )
    signals = signal_part.reshape(per_row, rows, 8, width)[:, :, 0]
    signals = signals.transpose(1, 0, 2).reshape(rows, rows_in)
    mod_rows = mod_grad_all[:, :, 0]
    mod_rows = mod_rows.reshape(rows, LAYERS, 6, width)
    grad_w_mod = sum(
        signals[r][None, :, None, None] * mod_rows[r][:, None] for r in range(rows)
    )
    grad_b_mod = jnp.sum(mod_rows, 0)
    grad_signal = lax.dynamic_slice(
        grad_signal[:1], (0, lax.axis_index("col") % per_row * width), (1, width)
    )
    grad_cond = jax.vjp(jax.nn.silu, cond_float)[1](grad_signal)[0]
    bias_sum = bias_sum[0].reshape(LAYERS, -1)
    return (
        output,
        grad.T,
        grad_cond,
        grad_w_mod,
        grad_b_mod,
        jnp.stack(grads_qkv).reshape(LAYERS, rows_in, 3, width),
        bias_sum[:, : 2 * width].reshape(LAYERS, 2, width),
        jnp.stack([one.T for one in grads_out]),
        bias_sum[:, 2 * width : 3 * width],
        jnp.stack(grads_one),
        bias_sum[:, 4 * width :],
        jnp.stack([one.T for one in grads_two]),
        bias_sum[:, 3 * width : 4 * width],
    )


def solution(mesh):
    in_specs = (
        P("row", "col"),
        P("row", "col"),
        P(None, "row", None, "col"),
        P(None, None, "col"),
        P(None, "row", None, "col"),
        P(None, None, "col"),
        P(None, "row", "col"),
        P(None, "col"),
        P(None, "row", "col"),
        P(None, "col"),
        P(None, "row", "col"),
        P(None, "col"),
        P("row", "col"),
    )
    out_specs = (
        P("row", "col"),
        P("row", "col"),
        P("row", "col"),
        P(None, "row", None, "col"),
        P(None, None, "col"),
        P(None, "row", None, "col"),
        P(None, None, "col"),
        P(None, "row", "col"),
        P(None, "col"),
        P(None, "row", "col"),
        P(None, "col"),
        P(None, "row", "col"),
        P(None, "col"),
    )
    return jax.shard_map(
        functools.partial(per_device, (mesh.shape["row"], mesh.shape["col"])),
        mesh=mesh,
        in_specs=in_specs,
        out_specs=out_specs,
        check_vma=False,
    )
```
